32 devices in a mesh: chan: 8 (over z, x), win: 4 (over y, core).
Axes of the slice: x: 2, y: 2, z: 4, core: 2. Of those that a mesh axis runs over, the one named last changes fastest.
Arguments:
- spectra: bfloat16 [64, 1024, 1024], P('win', 'chan'), may hold values from -400 to 400
- valid: int32 [64], P('win'), may hold values 0 or 1
- sources: int32 [32], replicated, may hold values from 0 to 1023, as said below
Outputs:
- correlations: bfloat16 [1024, 32, 512], P(('chan', 'win'))
The draws below stay inside these ranges and needn't reach their ends.
Inputs may be any that keep to these rules, and one draw needn't show every extreme that they name: `sources`: each entry is a receiver channel; entries may repeat.
All inputs are finite; a program needn't handle non-finite values. No bound on the sum of `valid` on one device may be relied on, other than what follows from the above.
Results may differ from the reference program's by a relative error of at most 0.023.
Values may be sent and summed in bfloat16 or wider, within the bound.
No kernel may reach another device: no remote copies, remote signals or barrier semaphores. Data moves between devices by JAX's collectives and lax.ppermute only.
A program may use at most 128 MiB of HBM per device.

```python
import jax
import jax.numpy as jnp
from jax import lax

FREQS = 512
LAGS = 512
SMOOTH = 21
SOURCES = 32
W_DEV = 16
C_DEV = 128
WINDOWS = 64
CHANNELS = 1024
N_WIN = 4


def draw_spectra(key, part):
    key = jax.random.fold_in(key, 11)
    key_vals, key_chan, key_freq = jax.random.split(key, 3)
    shape = (WINDOWS, CHANNELS, 2 * FREQS)
    values = jnp.clip(jax.random.normal(key_vals, shape, jnp.float32), -4.0, 4.0)
    chan_scale = jnp.exp(jax.random.uniform(key_chan, (1, CHANNELS, 1), jnp.float32, 0.0, jnp.log(10.0)))
    freq_scale = jnp.exp(jax.random.uniform(key_freq, (1, 1, FREQS), jnp.float32, 0.0, jnp.log(10.0)))
    freq_scale = jnp.concatenate([freq_scale, freq_scale], axis=-1)
    return (values * chan_scale * freq_scale).astype(jnp.bfloat16)


def draw_sources(key, part):
    key = jax.random.fold_in(key, 23)
    key_ids, key_perm = jax.random.split(key)
    chosen = jax.random.randint(key_ids, (SOURCES,), 0, CHANNELS, jnp.int32)
    order = jax.random.permutation(key_perm, SOURCES)
    chosen = chosen.at[order[0]].set(CHANNELS - 1)
    chosen = chosen.at[order[1]].set(0)
    return chosen.astype(jnp.int32)


def plant(drawn, rng, smallest, high):
    shape = drawn.shape
    place = [jax.random.randint(jax.random.fold_in(rng, axis), (), 0, shape[axis]) for axis in range(len(shape))]
    drawn = drawn.at[tuple(place)].set(smallest)
    longest = shape.index(max(shape))
    place[longest] = (place[longest] + 1) % shape[longest]
    return drawn.at[tuple(place)].set(high)


def setup_inputs(seed: int = 0) -> dict:
    key_of = jax.random.split(jax.random.key(seed), 4)
    return {
        "spectra": draw_spectra(jax.random.fold_in(key_of[3], 71), 0),
        "valid": plant((jax.random.randint(key_of[1], (WINDOWS,), 0, 4) < 3).astype(jnp.int32), jax.random.fold_in(key_of[1], 1), 0, 1),
        "sources": draw_sources(jax.random.fold_in(key_of[3], 71), 0),
    }


EPSILON = 1e-06

def whiten_window(window_data):
    values = window_data.astype(jnp.float32)
    magnitude = jnp.sqrt(values[:, :FREQS] * values[:, :FREQS] + values[:, FREQS:] * values[:, FREQS:])
    padded = jnp.pad(magnitude, ((0, 0), (SMOOTH, SMOOTH)))
    ones_pad = jnp.pad(jnp.ones((FREQS,), jnp.float32), (SMOOTH, SMOOTH))
    smoothed = jnp.zeros_like(magnitude)
    entries = jnp.zeros((FREQS,), jnp.float32)
    for shift_at in range(2 * SMOOTH + 1):
        smoothed = smoothed + padded[:, shift_at:shift_at + FREQS]
        entries = entries + ones_pad[shift_at:shift_at + FREQS]
    spatial = jnp.roll(smoothed, 1, axis=0) + smoothed + jnp.roll(smoothed, -1, axis=0)
    divisor = spatial / (3.0 * entries)[None, :] + EPSILON
    return (values / jnp.concatenate([divisor, divisor], axis=-1)).astype(jnp.bfloat16)

def reference(spectra, valid, sources):
    whitened = lax.map(whiten_window, spectra)
    picked = jnp.transpose(whitened[:, sources, :], (1, 0, 2))
    source_rows = picked * valid.astype(jnp.bfloat16)[None, :, None]
    src_float = source_rows.astype(jnp.float32)
    src_both = jnp.concatenate([src_float[..., :FREQS], src_float[..., FREQS:]], axis=1)
    block_rows = C_DEV // N_WIN
    lag_scale = 0.25 / jnp.sqrt(jnp.float32(FREQS * W_DEV))

    def one_block(block_id):
        received = lax.dynamic_slice_in_dim(whitened, block_id * block_rows, block_rows, 1).astype(jnp.float32)
        recv_real = received[..., :FREQS]
        recv_imag = received[..., FREQS:]
        real_rhs = jnp.concatenate([recv_real, recv_imag], axis=0)
        imag_rhs = jnp.concatenate([recv_imag, -recv_real], axis=0)
        real_part = jnp.einsum('swf,wcf->csf', src_both, real_rhs)
        imag_part = jnp.einsum('swf,wcf->csf', src_both, imag_rhs)
        stacked = jnp.concatenate([real_part, imag_part], axis=-1).astype(jnp.bfloat16).astype(jnp.float32)
        spectrum = stacked[..., :FREQS] + 1j * stacked[..., FREQS:]
        spectrum = jnp.pad(spectrum, ((0, 0), (0, 0), (0, 1)))
        full_lags = jnp.fft.irfft(spectrum, n=2 * FREQS, axis=-1) * (2 * FREQS) * lag_scale
        centred = jnp.concatenate([full_lags[..., 2 * FREQS - LAGS // 2:], full_lags[..., :LAGS // 2]], axis=-1)
        return centred.astype(jnp.bfloat16)
    blocks = lax.map(one_block, jnp.arange(CHANNELS // block_rows).astype(jnp.int32))
    return blocks.reshape(CHANNELS, SOURCES, LAGS)
```

```python
import functools
import math

import jax
import jax.numpy as jnp
from jax import lax
from jax.experimental import pallas as pl
from jax.experimental.pallas import tpu as pltpu
from jax.sharding import PartitionSpec as P

LAGS = 512
SMOOTH = 21
EPSILON = 1e-06
CHUNKS = 2
F32 = jnp.float32
BF16 = jnp.bfloat16
MIB = 1024 * 1024
LANES = 128


def xor_pairs(count, mask):
    return [(i, i ^ mask) for i in range(count)]


def place(blocks):
    if blocks != 8:
        return 0, 0
    at = lax.axis_index("chan")
    return at % 2, at // 2


def whiten_kernel(blocks, src_ref, valid_ref, spec_ref, low_ref, high_ref, white_ref, *rest):
    picks, (band, sel, held) = rest[:-3], rest[-3:]
    step = pl.program_id(0)
    chans, width = white_ref.shape[1:]
    freqs = width // 2
    sources = src_ref.shape[0]
    windows = held.shape[1] // sources

    @pl.when(step == 0)
    def _():
        row = lax.broadcasted_iota(jnp.int32, (freqs, freqs), 0)
        col = lax.broadcasted_iota(jnp.int32, (freqs, freqs), 1)
        band[...] = jnp.where(jnp.abs(row - col) <= SMOOTH, 1.0, 0.0).astype(BF16)
        x, z = place(blocks)
        offset = lax.axis_index("chan") * chans
        lane = lax.broadcasted_iota(jnp.int32, (1, chans), 1)
        per_chunk = sources // CHUNKS
        quarter = per_chunk // 8
        for r in range(sources):
            chunk, rest_r = divmod(r, per_chunk)
            half, rest_r = divmod(rest_r, 4 * quarter)
            part, i = divmod(rest_r, quarter)
            at = chunk * per_chunk + (x ^ half) * 4 * quarter + (z ^ part) * quarter + i
            sel[r : r + 1, :] = jnp.where(lane == src_ref[at] - offset, 1.0, 0.0)

    values = spec_ref[0].astype(F32)
    real, imag = values[:, :freqs], values[:, freqs:]
    magnitude = jnp.sqrt(real * real + imag * imag)

    def edge(ref):
        v = ref[0].astype(F32)
        return jnp.sqrt(v[:, :freqs] * v[:, :freqs] + v[:, freqs:] * v[:, freqs:])

    row = lax.broadcasted_iota(jnp.int32, (chans, freqs), 0)
    before = jnp.where(row == 0, edge(low_ref), pltpu.roll(magnitude, 1, 0))
    after = jnp.where(row == chans - 1, edge(high_ref), pltpu.roll(magnitude, chans - 1, 0))
    triple = (before + magnitude + after).astype(BF16)
    spatial = jnp.dot(triple, band[...], preferred_element_type=F32)
    f = lax.broadcasted_iota(jnp.int32, (1, freqs), 1)
    entries = jnp.minimum(f, SMOOTH) + jnp.minimum(freqs - 1 - f, SMOOTH) + 1
    inverse = 1.0 / (spatial * (1.0 / (3.0 * entries.astype(F32))) + EPSILON)
    white = jnp.concatenate([real * inverse, imag * inverse], axis=1).astype(BF16)
    white_ref[0] = white
    keep = (sel[...] * valid_ref[step].astype(F32)).astype(BF16)
    picked = jnp.dot(keep, white, preferred_element_type=F32)
    for j in range(width // LANES):
        held[j, pl.ds(step, sources, stride=windows), :] = picked[:, j * LANES : (j + 1) * LANES]

    @pl.when(step == windows - 1)
    def _():
        rows = picks[0].shape[0]
        for i, pick in enumerate(picks):
            for s in range(rows):
                at = (i * rows + s) * windows
                for j in range(width // LANES):
                    pick[s, :, j * LANES : (j + 1) * LANES] = held[j, at : at + windows, :].astype(BF16)


def whiten(blocks, spectra, valid, sources, low, high):
    windows, chans, width = spectra.shape
    count = sources.shape[0]
    rows = count // CHUNKS // 2
    smem = pl.BlockSpec(memory_space=pltpu.SMEM)
    edge = pl.BlockSpec((1, 1, width), lambda w: (w, 0, 0))
    block = pl.BlockSpec((1, chans, width), lambda w: (w, 0, 0))
    pick = pl.BlockSpec((rows, windows, width), lambda w: (0, 0, 0))
    return pl.pallas_call(
        functools.partial(whiten_kernel, blocks),
        grid=(windows,),
        in_specs=[smem, smem, block, edge, edge],
        out_specs=[block] + [pick] * (2 * CHUNKS),
        out_shape=[jax.ShapeDtypeStruct(spectra.shape, BF16)]
        + [jax.ShapeDtypeStruct((rows, windows, width), BF16)] * (2 * CHUNKS),
        scratch_shapes=[
            pltpu.VMEM((width // 2, width // 2), BF16),
            pltpu.VMEM((count, chans), F32),
            pltpu.VMEM((width // LANES, count * windows, LANES), F32),
        ],
        compiler_params=pltpu.CompilerParams(vmem_limit_bytes=24 * MIB),
        name="whiten",
    )(sources, valid, spectra, low, high)


def turn_kernel(real_ref, imag_ref, out_ref, held):
    windows, chans, tile = real_ref.shape
    rows = 2 * windows
    for w in range(windows):
        re = real_ref[w].astype(F32).T
        im = imag_ref[w].astype(F32).T
        held[0, pl.ds(w, tile, stride=rows), :] = re
        held[0, pl.ds(windows + w, tile, stride=rows), :] = im
        held[1, pl.ds(w, tile, stride=rows), :] = im
        held[1, pl.ds(windows + w, tile, stride=rows), :] = -re
    out_ref[:, :, :chans] = held[0].astype(BF16).reshape(tile, rows, chans)
    out_ref[:, :, chans:] = held[1].astype(BF16).reshape(tile, rows, chans)


def turn(white):
    windows, chans, width = white.shape
    freqs = width // 2
    tile = 128
    tiles = freqs // tile
    return pl.pallas_call(
        turn_kernel,
        grid=(tiles,),
        in_specs=[
            pl.BlockSpec((windows, chans, tile), lambda j: (0, 0, j)),
            pl.BlockSpec((windows, chans, tile), lambda j: (0, 0, j + tiles)),
        ],
        out_specs=pl.BlockSpec((tile, 2 * windows, 2 * chans), lambda j: (j, 0, 0)),
        out_shape=jax.ShapeDtypeStruct((freqs, 2 * windows, 2 * chans), BF16),
        scratch_shapes=[pltpu.VMEM((2, tile * 2 * windows, chans), F32)],
        compiler_params=pltpu.CompilerParams(vmem_limit_bytes=32 * MIB),
        cost_estimate=pl.CostEstimate(flops=0, bytes_accessed=24 * MIB, transcendentals=0),
        name="turn",
    )(white, white)


def cross_kernel(parts, mine_ref, theirs_ref, turned_ref, table_ref, keep_ref, send_ref, vt, st):
    half, windows, width = mine_ref.shape
    freqs, depth, both = turned_ref.shape
    chans = both // 2
    rows = 2 * half
    tile = 128
    group = tile // depth
    for g in range(rows // group):
        pieces = []
        for s in range(g * group, (g + 1) * group):
            ref = mine_ref if s < half else theirs_ref
            v = ref[s % half].astype(F32)
            pieces += [v[:, :freqs], v[:, freqs:]]
        stack = jnp.concatenate(pieces, axis=0)
        for j in range(freqs // tile):
            t = stack[:, j * tile : (j + 1) * tile].T
            for i in range(group):
                turned_here = t if i == 0 else pltpu.roll(t, tile - i * depth, 1)
                vt[pl.ds(j * tile * rows + g * group + i, tile, stride=rows), :] = turned_here

    unroll = 16

    def step(i, carry):
        for k in range(unroll):
            f = i * unroll + k
            at = pl.multiple_of(f * rows, rows)
            lhs = vt[pl.ds(at, rows), 0:depth].astype(BF16)
            sums = jnp.dot(lhs, turned_ref[f], preferred_element_type=F32)
            st[0, pl.ds(at, rows), :] = sums[:, :chans]
            st[1, pl.ds(at, rows), :] = sums[:, chans:]
        return carry

    lax.fori_loop(0, freqs // unroll, step, 0)

    me = lax.axis_index("win")
    share = chans // parts

    def lags(p, carry):
        cols = []
        for s in (2 * p, 2 * p + 1):
            parts_of_s = [st[i, pl.ds(s, freqs, stride=rows), :].astype(BF16) for i in (0, 1)]
            cols.append(jnp.concatenate(parts_of_s, axis=0))
        out = jnp.dot(table_ref[...], jnp.concatenate(cols, axis=1), preferred_element_type=F32)
        for k in range(2):
            flat = out[:, k * chans : (k + 1) * chans].T.astype(BF16)
            for b in range(parts):
                slot = b ^ me
                value = flat[b * share : (b + 1) * share, :]

                @pl.when(slot % 2 == 0)
                def _():
                    keep_ref[slot // 2, 2 * p + k] = value

                @pl.when(slot % 2 == 1)
                def _():
                    send_ref[slot // 2, 2 * p + k] = value

        return carry

    lax.fori_loop(0, rows // 2, lags, 0)


def cross(parts, mine, theirs, turned, table):
    half, windows, width = mine.shape
    freqs, depth, both = turned.shape
    rows = 2 * half
    chans = both // 2
    lags = table.shape[0]
    shape = jax.ShapeDtypeStruct((parts // 2, rows, chans // parts, lags), BF16)
    whole = pl.BlockSpec(memory_space=pltpu.VMEM)
    return pl.pallas_call(
        functools.partial(cross_kernel, parts),
        in_specs=[whole] * 4,
        out_specs=[whole] * 2,
        out_shape=[shape] * 2,
        scratch_shapes=[
            pltpu.VMEM((freqs * rows, 128), F32),
            pltpu.VMEM((2, freqs * rows, chans), F32),
        ],
        compiler_params=pltpu.CompilerParams(vmem_limit_bytes=48 * MIB),
        cost_estimate=pl.CostEstimate(flops=8 * 10**9, bytes_accessed=16 * MIB, transcendentals=0),
        name="cross",
    )(mine, theirs, turned, table)


def finish_kernel(blocks, *refs):
    ins, (out_ref, held) = refs[:-2], refs[-2:]
    chans, sources, lags = out_ref.shape
    x, z = place(blocks)
    per_chunk = sources // CHUNKS
    quarter = per_chunk // 8
    for chunk in range(CHUNKS):
        own, came = ins[2 * chunk], ins[2 * chunk + 1]
        for r in range(per_chunk):
            half, rest_r = divmod(r, 4 * quarter)
            part, i = divmod(rest_r, quarter)
            at = chunk * per_chunk + (x ^ half) * 4 * quarter + (z ^ part) * quarter + i
            total = own[0, r].astype(F32) + came[0, r].astype(F32)
            for j in range(lags // LANES):
                held[j, pl.ds(at, chans, stride=sources), :] = total[:, j * LANES : (j + 1) * LANES]
    for c in range(chans):
        for j in range(lags // LANES):
            rows = held[j, c * sources : (c + 1) * sources, :]
            out_ref[c, :, j * LANES : (j + 1) * LANES] = rows.astype(BF16)


def finish(blocks, ins, sources):
    _, _, chans, lags = ins[0].shape
    whole = pl.BlockSpec(memory_space=pltpu.VMEM)
    return pl.pallas_call(
        functools.partial(finish_kernel, blocks),
        in_specs=[whole] * len(ins),
        out_specs=whole,
        out_shape=jax.ShapeDtypeStruct((chans, sources, lags), BF16),
        scratch_shapes=[pltpu.VMEM((lags // LANES, chans * sources, LANES), F32)],
        compiler_params=pltpu.CompilerParams(vmem_limit_bytes=24 * MIB),
        name="finish",
    )(*ins)


def spread(blocks, keep, send):
    if blocks != 8:
        return lax.psum(keep, "chan"), lax.psum(send, "chan")
    quarter = keep.shape[0] // 4
    across = xor_pairs(8, 1)
    total = keep + lax.ppermute(send, "chan", across)
    pieces = [total[p * quarter : (p + 1) * quarter] for p in range(4)]
    own = pieces[0]
    came = [lax.ppermute(pieces[p], "chan", xor_pairs(8, 2 * p)) for p in (1, 2, 3)]
    own = own + came[0] + came[1] + came[2]
    others = [lax.ppermute(own, "chan", xor_pairs(8, 2 * p)) for p in (1, 2, 3)]
    mine = jnp.concatenate([own] + others, axis=0)
    return mine, lax.ppermute(mine, "chan", across)


def lag_table(freqs, windows):
    freq_index = jnp.arange(freqs).astype(F32)[None, :]
    lag_shift = (jnp.arange(LAGS) - LAGS // 2).astype(F32)[:, None]
    phase_angle = math.pi * freq_index * lag_shift / freqs
    weights = jnp.where(freq_index == 0.0, 1.0, 2.0)
    lag_scale = 0.25 / math.sqrt(freqs * windows)
    return jnp.concatenate(
        [weights * jnp.cos(phase_angle) * lag_scale, -weights * jnp.sin(phase_angle) * lag_scale], axis=1
    ).astype(BF16)


def on_device(blocks, parts, spectra, valid, sources):
    windows, chans, width = spectra.shape
    freqs = width // 2
    forward = [(i, (i + 1) % blocks) for i in range(blocks)]
    backward = [(b, a) for a, b in forward]
    low = lax.ppermute(spectra[:, chans - 1 :, :], "chan", forward)
    high = lax.ppermute(spectra[:, :1, :], "chan", backward)
    white, *picks = whiten(blocks, spectra, valid, sources, low, high)
    table = lag_table(freqs, windows)
    turned = turn(white)
    ins = []
    for chunk in range(CHUNKS):
        mine, theirs = spread(blocks, picks[2 * chunk], picks[2 * chunk + 1])
        keep, send = cross(parts, mine, theirs, turned, table)
        total = keep + lax.ppermute(send, "win", xor_pairs(parts, 1))
        ins += [total[:1], lax.ppermute(total[1:], "win", xor_pairs(parts, 2))]
    return finish(blocks, ins, sources.shape[0])


def solution(mesh):
    return jax.shard_map(
        functools.partial(on_device, mesh.shape["chan"], mesh.shape["win"]),
        mesh=mesh,
        in_specs=(P("win", "chan", None), P("win"), P()),
        out_specs=P(("chan", "win"), None, None),
        check_vma=False,
    )
```

```python
import functools
import math

import jax
import jax.numpy as jnp
import ml_dtypes
import numpy as np
from jax import lax
from jax.experimental import pallas as pl
from jax.experimental.pallas import tpu as pltpu
from jax.sharding import PartitionSpec as P

LAGS = 512
SMOOTH = 21
EPSILON = 1e-06
CHUNKS = 2
LANES = 128
F32 = jnp.float32
BF16 = jnp.bfloat16
MIB = 1024 * 1024
SMEM = pl.BlockSpec(memory_space=pltpu.SMEM)
VMEM = pl.BlockSpec(memory_space=pltpu.VMEM)
ANY = pl.BlockSpec(memory_space=pl.ANY)


def cost(us):
    return pl.CostEstimate(flops=0, bytes_accessed=int(us * 3 * 10**6), transcendentals=0)


def call(kernel, ins, in_specs, outs, scratch, limit, us, name):
    return pl.pallas_call(
        kernel,
        in_specs=in_specs,
        out_specs=[VMEM] * len(outs),
        out_shape=[jax.ShapeDtypeStruct(shape, dtype) for shape, dtype in outs],
        scratch_shapes=scratch,
        compiler_params=pltpu.CompilerParams(vmem_limit_bytes=limit * MIB),
        cost_estimate=cost(us),
        name=name,
    )(*ins)


def xor_pairs(count, mask):
    return [(i, i ^ mask) for i in range(count)]


def place(blocks):
    if blocks != 8:
        return 0, 0
    at = lax.axis_index("chan")
    return at % 2, at // 2


def source_at(blocks, r, per_chunk):
    x, z = place(blocks)
    quarter = per_chunk // 8
    chunk, r = divmod(r, per_chunk)
    half, r = divmod(r, 4 * quarter)
    part, i = divmod(r, quarter)
    return chunk * per_chunk + (x ^ half) * 4 * quarter + (z ^ part) * quarter + i


def amplitude(values):
    freqs = values.shape[-1] // 2
    real, imag = values[:, :freqs], values[:, freqs:]
    return jnp.sqrt(real * real + imag * imag)


def bin_share(freqs):
    f = lax.broadcasted_iota(jnp.int32, (1, freqs), 1)
    entries = jnp.minimum(f, SMOOTH) + jnp.minimum(freqs - 1 - f, SMOOTH) + 1
    return 1.0 / (3.0 * entries.astype(F32))


def whitened_rows(values, triple, band, share):
    freqs = triple.shape[-1]
    spatial = jnp.dot(triple.astype(BF16), band, preferred_element_type=F32)
    inverse = 1.0 / (spatial * share + EPSILON)
    return jnp.concatenate([values[:, :freqs] * inverse, values[:, freqs:] * inverse], axis=1).astype(BF16)


def whiten_kernel(blocks, src_ref, valid_ref, spec_ref, white_ref, held, band, part_ref, raw_ref, buf, sel, sems):
    windows, chans, width = white_ref.shape
    freqs = width // 2
    sources = src_ref.shape[0]
    pitch = windows + 8

    def fetch(w):
        return pltpu.make_async_copy(spec_ref.at[w], buf.at[w], sems.at[w])

    for w in range(windows):
        fetch(w).start()
    row = lax.broadcasted_iota(jnp.int32, (freqs, freqs), 0)
    col = lax.broadcasted_iota(jnp.int32, (freqs, freqs), 1)
    band[...] = jnp.where(jnp.abs(row - col) <= SMOOTH, 1.0, 0.0).astype(BF16)
    offset = lax.axis_index("chan") * chans
    lane = lax.broadcasted_iota(jnp.int32, (1, chans), 1)
    inner = jnp.where((lane > 0) & (lane < chans - 1), 1.0, 0.0)
    for r in range(sources):
        at = src_ref[source_at(blocks, r, sources // CHUNKS)] - offset
        sel[r : r + 1, :] = jnp.where(lane == at, inner, 0.0)
    share = bin_share(freqs)

    def one(w, carry):
        fetch(w).wait()
        values = buf[w].astype(F32)
        magnitude = amplitude(values)
        triple = pltpu.roll(magnitude, 1, 0) + magnitude + pltpu.roll(magnitude, chans - 1, 0)
        white = whitened_rows(values, triple, band[...], share)
        white_ref[w] = white
        part_ref[0, pl.ds(w, 1), :] = magnitude[0:1] + magnitude[1:2]
        part_ref[1, pl.ds(w, 1), :] = magnitude[chans - 2 : chans - 1] + magnitude[chans - 1 :]
        raw_ref[0, pl.ds(w, 1), :] = values[0:1]
        raw_ref[1, pl.ds(w, 1), :] = values[chans - 1 :]
        keep = (sel[...] * valid_ref[w].astype(F32)).astype(BF16)
        picked = jnp.dot(keep, white, preferred_element_type=F32)
        for j in range(width // LANES):
            held[j, pl.ds(w, sources, stride=pitch), :] = picked[:, j * LANES : (j + 1) * LANES]
        return carry

    lax.fori_loop(0, windows, one, 0, unroll=2)


def whiten(blocks, spectra, valid, sources):
    windows, chans, width = spectra.shape
    count = sources.shape[0]
    return call(
        functools.partial(whiten_kernel, blocks),
        (sources, valid, spectra),
        [SMEM, SMEM, ANY],
        [
            (spectra.shape, BF16),
            ((width // LANES, count * (windows + 8), LANES), F32),
            ((width // 2, width // 2), BF16),
            ((2, windows, width // 2), F32),
            ((2, windows, width), F32),
        ],
        [
            pltpu.VMEM(spectra.shape, BF16),
            pltpu.VMEM((count, chans), F32),
            pltpu.SemaphoreType.DMA((windows,)),
        ],
        24,
        6,
        "whiten",
    )


def edges_kernel(blocks, chans, src_ref, valid_ref, low_ref, high_ref, held, band, part_ref, raw_ref, *outs):
    picks, edge_ref = outs[:-1], outs[-1]
    windows, width = raw_ref.shape[1:]
    freqs = width // 2
    sources = src_ref.shape[0]
    pitch = windows + 8
    share = bin_share(freqs)
    row = lax.broadcasted_iota(jnp.int32, (windows, 1), 0)
    valid = jnp.zeros((windows, 1), F32)
    for w in range(windows):
        valid = valid + jnp.where(row == w, valid_ref[w].astype(F32), 0.0)
    entering = []
    for k, ref in enumerate((low_ref, high_ref)):
        beside = jnp.concatenate([ref[w] for w in range(windows)], axis=0).astype(F32)
        white = whitened_rows(raw_ref[k], part_ref[k] + amplitude(beside), band[...], share).astype(F32)
        edge_ref[k] = white
        entering.append(white * valid)
    offset = lax.axis_index("chan") * chans
    rows = picks[0].shape[0]
    for r in range(sources):
        at = src_ref[source_at(blocks, r, sources // CHUNKS)] - offset
        first = (at == 0).astype(F32)
        last = (at == chans - 1).astype(F32)
        for j in range(width // LANES):
            lanes = slice(j * LANES, (j + 1) * LANES)
            value = held[j, r * pitch : r * pitch + windows, :]
            value = value + first * entering[0][:, lanes] + last * entering[1][:, lanes]
            picks[r // rows][r % rows, :, lanes] = value.astype(BF16)


def edges(blocks, chans, valid, sources, low, high, held, band, part, raw):
    _, windows, width = raw.shape
    rows = sources.shape[0] // CHUNKS // 2
    return call(
        functools.partial(edges_kernel, blocks, chans),
        (sources, valid, low, high, held, band, part, raw),
        [SMEM, SMEM] + [VMEM] * 6,
        [((rows, windows, width), BF16)] * (2 * CHUNKS) + [(raw.shape, F32)],
        [],
        16,
        1,
        "edges",
    )


def turn_kernel(first, white_ref, edge_ref, out_ref, held):
    windows, chans, width = white_ref.shape
    tile = LANES
    pitch = 2 * windows + 8
    for block in range(out_ref.shape[0] // tile):
        for w in range(windows):
            for half in range(2):
                at = half * (width // 2) + (first + block) * tile
                lanes = slice(at, at + tile)
                body = white_ref[w, :, lanes].astype(F32)
                row = lax.broadcasted_iota(jnp.int32, (8, tile), 0)
                top = jnp.where(row == 0, edge_ref[0, w : w + 1, lanes], body[:8])
                bottom = jnp.where(row == 7, edge_ref[1, w : w + 1, lanes], body[chans - 8 :])
                body = jnp.concatenate([top, body[8 : chans - 8], bottom], axis=0)
                held[pl.ds(half * windows + w, tile, stride=pitch), :] = body.T
        for f in range(tile):
            out_ref[block * tile + f] = held[f * pitch : f * pitch + 2 * windows, :].astype(BF16)


def turn(white, edge, first, tiles):
    windows, chans, width = white.shape
    return call(
        functools.partial(turn_kernel, first),
        (white, edge),
        [VMEM, VMEM],
        [((tiles * LANES, 2 * windows, chans), BF16)],
        [pltpu.VMEM((LANES * (2 * windows + 8), chans), F32)],
        16,
        4,
        "turn",
    )[0]


def add_parts_kernel(keep_ref, came_ref, after_ref, *outs):
    rows = outs[0].shape[0]
    for p, out in enumerate(outs):
        out[...] = keep_ref[p * rows : (p + 1) * rows] + came_ref[p * rows : (p + 1) * rows]


def add_parts(keep, came, after):
    rows, windows, width = keep.shape
    return call(
        add_parts_kernel,
        (keep, came, after),
        [VMEM, VMEM, ANY],
        [((rows // 4, windows, width), BF16)] * 4,
        [],
        8,
        0.2,
        "add_parts",
    )


def add_four_kernel(a_ref, b_ref, c_ref, d_ref, after_ref, out_ref):
    out_ref[...] = a_ref[...] + b_ref[...] + c_ref[...] + d_ref[...]


def add_four(pieces, after):
    return call(
        add_four_kernel,
        (*pieces, after),
        [VMEM] * 4 + [ANY],
        [(pieces[0].shape, BF16)],
        [],
        8,
        0.2,
        "add_four",
    )[0]


def cross_kernel(parts, mine_ref, theirs_ref, low_ref, high_ref, cos_ref, sin_ref, after_ref, keep_ref, send_ref, vt, st):
    half, windows, width = mine_ref.shape
    held_freqs, depth, chans = low_ref.shape
    freqs = width // 2
    rows = 2 * half
    pitch = rows + 8
    tile = LANES
    group = tile // depth
    for g in range(rows // group):
        pieces = []
        for s in range(g * group, (g + 1) * group):
            ref = mine_ref if s < half else theirs_ref
            v = ref[s % half].astype(F32)
            pieces += [v[:, :freqs], v[:, freqs:]]
        stack = jnp.concatenate(pieces, axis=0)
        for j in range(freqs // tile):
            t = stack[:, j * tile : (j + 1) * tile].T
            for i in range(group):
                moved = t if i == 0 else pltpu.roll(t, tile - i * depth, 1)
                vt[pl.ds(j * tile * pitch + g * group + i, tile, stride=pitch), :] = moved

    unroll = 64
    for which, ref in enumerate((low_ref, high_ref)):

        def step(i, carry):
            for k in range(unroll):
                f = i * unroll + k
                at = pl.multiple_of((which * held_freqs + f) * pitch, 8)
                lhs = vt[pl.ds(at, rows), 0:depth].astype(BF16)
                x = ref[f]
                crossed = jnp.concatenate([x[windows:], -x[:windows]], axis=0)
                sums = jnp.dot(lhs, jnp.concatenate([x, crossed], axis=1), preferred_element_type=F32)
                st[0, pl.ds(at, rows), :] = sums[:, :chans]
                st[1, pl.ds(at, rows), :] = sums[:, chans:]
            return carry

        lax.fori_loop(0, held_freqs // unroll, step, 0)

    me = lax.axis_index("win")
    share = chans // parts
    lags = keep_ref.shape[-1]
    last_row = lax.broadcasted_iota(jnp.int32, (8, 1), 0) == 7

    def transform(p, carry):
        real, imag = [
            jnp.concatenate([st[i, pl.ds(2 * p + k, freqs, stride=pitch), :].astype(BF16) for k in (0, 1)], axis=1)
            for i in (0, 1)
        ]
        even = jnp.dot(cos_ref[...], real, preferred_element_type=F32)
        odd = jnp.dot(sin_ref[...], imag, preferred_element_type=F32)
        tail = odd[lags // 2 - 8 :] + jnp.where(last_row, even[lags // 2 : lags // 2 + 1], 0.0)
        out = jnp.concatenate([even[: lags // 2], odd[: lags // 2 - 8], tail], axis=0)
        for k in range(2):
            flat = out[:, k * chans : (k + 1) * chans].T.astype(BF16)
            for b in range(parts):
                slot = b ^ me
                value = flat[b * share : (b + 1) * share, :]

                @pl.when(slot % 2 == 0)
                def _():
                    keep_ref[slot // 2, 2 * p + k] = value

                @pl.when(slot % 2 == 1)
                def _():
                    send_ref[slot // 2, 2 * p + k] = value

        return carry

    lax.fori_loop(0, rows // 2, transform, 0)


def cross(parts, mine, theirs, turned, tables, after):
    half, windows, width = mine.shape
    chans = turned[0].shape[-1]
    rows = 2 * half
    held = width // 2 * (rows + 8)
    return call(
        functools.partial(cross_kernel, parts),
        (mine, theirs, *turned, *tables, after),
        [VMEM] * 6 + [ANY],
        [((parts // 2, rows, chans // parts, LAGS), BF16)] * 2,
        [pltpu.VMEM((held, LANES), F32), pltpu.VMEM((2, held, chans), F32)],
        32,
        7,
        "cross",
    )


def unfold_kernel(blocks, chunk, own_ref, came_ref, mix_ref, *rest):
    earlier, (out_ref, held) = rest[:-2], rest[-2:]
    rows, chans, lags = own_ref.shape[1:]
    pitch = rows + 8
    total = jnp.zeros((rows * chans, lags), F32)
    for ref in (own_ref, came_ref):
        flat = ref[...].reshape(rows * chans, lags)
        total = total + jnp.dot(flat, mix_ref[...], preferred_element_type=F32)
    for r in range(rows):
        at = source_at(blocks, r, rows)
        for j in range(lags // LANES):
            held[j, pl.ds(at, chans, stride=pitch), :] = total[r * chans : (r + 1) * chans, j * LANES : (j + 1) * LANES]
    first = out_ref.shape[1] - rows
    for c in range(chans):
        if earlier:
            out_ref[c, :first, :] = earlier[0][c]
        for j in range(lags // LANES):
            lanes = slice(j * LANES, (j + 1) * LANES)
            out_ref[c, first:, lanes] = held[j, c * pitch : c * pitch + rows, :].astype(BF16)


def unfold(blocks, own, came, mix, earlier):
    _, rows, chans, lags = own.shape
    return call(
        functools.partial(unfold_kernel, blocks, len(earlier)),
        (own, came, mix, *earlier),
        [VMEM] * (3 + len(earlier)),
        [((chans, rows * (1 + len(earlier)), lags), BF16)],
        [pltpu.VMEM((lags // LANES, chans * (rows + 8), LANES), F32)],
        16,
        1.5,
        "unfold",
    )[0]


def exchange_x(blocks, keep, send):
    return lax.ppermute(send, "chan", xor_pairs(blocks, 1))


def spread(blocks, keep, send, after):
    if blocks != 8:
        return lax.psum(keep, "chan"), lax.psum(send, "chan")
    across = xor_pairs(8, 1)
    pieces = add_parts(keep, lax.ppermute(send, "chan", across), after[0])
    came = [lax.ppermute(pieces[p], "chan", xor_pairs(8, 2 * p)) for p in (1, 2, 3)]
    own = add_four([pieces[0]] + came, after[1])
    others = [lax.ppermute(own, "chan", xor_pairs(8, 2 * p)) for p in (1, 2, 3)]
    mine = jnp.concatenate([own] + others, axis=0)
    return mine, lax.ppermute(mine, "chan", across)


def lag_tables(freqs, windows):
    half = LAGS // 2
    f = np.arange(freqs)[None, :]
    scale = np.where(f == 0, 1.0, 2.0) * 0.25 / math.sqrt(freqs * windows)
    u = np.arange(half + 16)[:, None]
    cos = np.where(u <= half, scale * np.cos(math.pi * (f * u % (2 * freqs)) / freqs), 0.0)
    u = np.arange(1, half + 1)[:, None]
    sin = -scale * np.sin(math.pi * (f * u % (2 * freqs)) / freqs) * np.where(u == half, -1.0, 1.0)
    return jnp.asarray(cos.astype(ml_dtypes.bfloat16)), jnp.asarray(sin.astype(ml_dtypes.bfloat16))


def lag_mix():
    half = LAGS // 2
    mix = np.zeros((LAGS, LAGS))
    u = np.arange(half)
    mix[u, half + u] = 1
    u = np.arange(1, half)
    mix[u, half - u] = 1
    mix[half - 1 + u, half + u] = 1
    mix[half - 1 + u, half - u] = -1
    mix[LAGS - 1, 0] = 1
    return jnp.asarray(mix.astype(ml_dtypes.bfloat16))


def on_device(blocks, parts, spectra, valid, sources):
    windows, chans, width = spectra.shape
    freqs = width // 2
    forward = [(i, (i + 1) % blocks) for i in range(blocks)]
    backward = [(b, a) for a, b in forward]
    low = lax.ppermute(spectra[:, chans - 1 :, :], "chan", forward)
    high = lax.ppermute(spectra[:, :1, :], "chan", backward)
    white, held, band, part, raw = whiten(blocks, spectra, valid, sources)
    *picks, edge = edges(blocks, chans, valid, sources, low, high, held, band, part, raw)
    tables = lag_tables(freqs, windows)
    mix = lag_mix()
    tiles = freqs // LANES // 2
    turned = [turn(white, edge, i * tiles, tiles) for i in range(2)]
    rows = [spread(blocks, picks[2 * c], picks[2 * c + 1], turned) for c in range(CHUNKS)]
    out, after = [], turned[0]
    for mine, theirs in rows:
        keep, send = cross(parts, mine, theirs, turned, tables, after)
        total = keep + lax.ppermute(send, "win", xor_pairs(parts, 1))
        after = total
        out = [unfold(blocks, total[:1], lax.ppermute(total[1:], "win", xor_pairs(parts, 2)), mix, out)]
    return out[0]


def solution(mesh):
    return jax.shard_map(
        functools.partial(on_device, mesh.shape["chan"], mesh.shape["win"]),
        mesh=mesh,
        in_specs=(P("win", "chan", None), P("win"), P()),
        out_specs=P(("chan", "win"), None, None),
        check_vma=False,
    )
```

```python
import functools
import math

import jax
import jax.numpy as jnp
import ml_dtypes
import numpy as np
from jax import lax
from jax.experimental import pallas as pl
from jax.experimental.pallas import tpu as pltpu
from jax.sharding import PartitionSpec as P

LAGS = 512
SMOOTH = 21
EPSILON = 1e-06
CHUNKS = 2
LANES = 128
F32 = jnp.float32
BF16 = jnp.bfloat16
MIB = 1024 * 1024
SMEM = pl.BlockSpec(memory_space=pltpu.SMEM)
VMEM = pl.BlockSpec(memory_space=pltpu.VMEM)
ANY = pl.BlockSpec(memory_space=pl.ANY)
HBM = pl.BlockSpec(memory_space=pltpu.HBM)


def call(kernel, ins, in_specs, outs, scratch, limit, name, after=()):
    count = len(ins)

    def body(*refs):
        kernel(*refs[:count], *refs[count + len(after) :])

    return pl.pallas_call(
        body,
        in_specs=[*in_specs] + [ANY] * len(after),
        out_specs=[VMEM] * len(outs),
        out_shape=[jax.ShapeDtypeStruct(shape, dtype) for shape, dtype in outs],
        scratch_shapes=scratch,
        compiler_params=pltpu.CompilerParams(vmem_limit_bytes=limit * MIB),
        cost_estimate=pl.CostEstimate(flops=0, bytes_accessed=16, transcendentals=0),
        name=name,
    )(*ins, *after)


def xor_pairs(count, mask):
    return [(i, i ^ mask) for i in range(count)]


def place(blocks):
    if blocks != 8:
        return 0, 0
    at = lax.axis_index("chan")
    return at % 2, at // 2


def source_at(blocks, r, per_chunk):
    x, z = place(blocks)
    quarter = per_chunk // 8
    chunk, r = divmod(r, per_chunk)
    half, r = divmod(r, 4 * quarter)
    part, i = divmod(r, quarter)
    return chunk * per_chunk + (x ^ half) * 4 * quarter + (z ^ part) * quarter + i


def amplitude(values):
    freqs = values.shape[-1] // 2
    real, imag = values[:, :freqs], values[:, freqs:]
    square = real * real + imag * imag
    return square * lax.rsqrt(jnp.maximum(square, 1e-36))


def bin_share(freqs):
    f = lax.broadcasted_iota(jnp.int32, (1, freqs), 1)
    entries = jnp.minimum(f, SMOOTH) + jnp.minimum(freqs - 1 - f, SMOOTH) + 1
    return 1.0 / (3.0 * entries.astype(F32))


def inverse_divisor(triple, band, share):
    divisor = jnp.dot(triple, band, preferred_element_type=F32) * share + EPSILON
    near = pl.reciprocal(divisor, approx=True)
    return near * (2.0 - divisor * near)


def whiten_kernel(spec_ref, white_ref, band, part_ref, raw_ref, buf, tri, inv, sems):
    windows, chans, width = buf.shape
    freqs = width // 2
    pitch = chans + 8
    together = tri.shape[0] // chans

    def fetch(w):
        return pltpu.make_async_copy(spec_ref.at[w], buf.at[w], sems.at[w])

    for w in range(windows):
        fetch(w).start()
    row = lax.broadcasted_iota(jnp.int32, (freqs, freqs), 0)
    col = lax.broadcasted_iota(jnp.int32, (freqs, freqs), 1)
    band[...] = jnp.where(jnp.abs(row - col) <= SMOOTH, 1.0, 0.0).astype(BF16)
    share = bin_share(freqs)

    def some(i, carry):
        for k in range(together):
            w = i * together + k
            fetch(w).wait()
            values = buf[w].astype(F32)
            magnitude = amplitude(values)
            triple = pltpu.roll(magnitude, 1, 0) + magnitude + pltpu.roll(magnitude, chans - 1, 0)
            tri[k * chans : (k + 1) * chans, :] = triple.astype(BF16)
            part_ref[0, pl.ds(w, 1), :] = magnitude[0:1] + magnitude[1:2]
            part_ref[1, pl.ds(w, 1), :] = magnitude[chans - 2 : chans - 1] + magnitude[chans - 1 :]
            raw_ref[0, pl.ds(w, 1), :] = values[0:1]
            raw_ref[1, pl.ds(w, 1), :] = values[chans - 1 :]
        inv[...] = inverse_divisor(tri[...], band[...], share)
        for k in range(together):
            w = i * together + k
            at = pl.multiple_of(w * pitch, 8)
            for j in range(width // LANES):
                values = buf[w, :, j * LANES : (j + 1) * LANES].astype(F32)
                first = j * LANES % freqs
                factor = inv[k * chans : (k + 1) * chans, first : first + LANES]
                white_ref[j, pl.ds(at, chans), :] = values * factor
        return carry

    lax.fori_loop(0, windows // together, some, 0)


def whiten(spectra):
    windows, chans, width = spectra.shape
    freqs = width // 2
    together = 4
    return call(
        whiten_kernel,
        (spectra,),
        [HBM],
        [
            ((width // LANES, windows * (chans + 8), LANES), F32),
            ((freqs, freqs), BF16),
            ((2, windows, freqs), F32),
            ((2, windows, width), F32),
        ],
        [
            pltpu.VMEM(spectra.shape, BF16),
            pltpu.VMEM((together * chans, freqs), BF16),
            pltpu.VMEM((together * chans, freqs), F32),
            pltpu.SemaphoreType.DMA((windows,)),
        ],
        28,
        "whiten",
    )


def edges_kernel(blocks, chans, src_ref, valid_ref, low_ref, high_ref, white_ref, band, part_ref, raw_ref, *outs):
    picks, edge_ref = outs[:-1], outs[-1]
    windows, width = raw_ref.shape[1:]
    freqs = width // 2
    sources = src_ref.shape[0]
    pitch = chans + 8
    share = bin_share(freqs)
    row = lax.broadcasted_iota(jnp.int32, (windows, 1), 0)
    valid = jnp.zeros((windows, 1), F32)
    for w in range(windows):
        valid = valid + jnp.where(row == w, valid_ref[w].astype(F32), 0.0)
    for k, ref in enumerate((low_ref, high_ref)):
        beside = jnp.concatenate([ref[w] for w in range(windows)], axis=0).astype(F32)
        triple = (part_ref[k] + amplitude(beside)).astype(BF16)
        inverse = inverse_divisor(triple, band[...], share)
        edge_ref[k] = raw_ref[k] * jnp.concatenate([inverse, inverse], axis=1)
    offset = lax.axis_index("chan") * chans
    rows = picks[0].shape[0]
    for r in range(sources):
        at = src_ref[source_at(blocks, r, sources // CHUNKS)] - offset
        inner = valid * ((at > 0) & (at < chans - 1)).astype(F32)
        first = valid * (at == 0).astype(F32)
        last = valid * (at == chans - 1).astype(F32)
        row_at = jnp.clip(at, 0, chans - 1)
        for j in range(width // LANES):
            lanes = slice(j * LANES, (j + 1) * LANES)
            value = inner * white_ref[j, pl.ds(row_at, windows, stride=pitch), :]
            value = value + first * edge_ref[0, :, lanes] + last * edge_ref[1, :, lanes]
            picks[r // rows][r % rows, :, lanes] = value.astype(BF16)


def edges(blocks, chans, valid, sources, low, high, white, band, part, raw):
    _, windows, width = raw.shape
    rows = sources.shape[0] // CHUNKS // 2
    return call(
        functools.partial(edges_kernel, blocks, chans),
        (sources, valid, low, high, white, band, part, raw),
        [SMEM, SMEM] + [VMEM] * 6,
        [((rows, windows, width), BF16)] * (2 * CHUNKS) + [(raw.shape, F32)],
        [],
        8,
        "edges",
    )


def turn_kernel(first, white_ref, edge_ref, out_ref, held):
    _, windows, width = edge_ref.shape
    chans = out_ref.shape[-1]
    tile = LANES
    pitch = 2 * windows + 8
    row = lax.broadcasted_iota(jnp.int32, (8, tile), 0)
    for block in range(out_ref.shape[0] // tile):
        for w in range(windows):
            for half in range(2):
                j = half * (width // 2 // tile) + first + block
                lanes = slice(j * tile, (j + 1) * tile)
                at = w * (chans + 8)
                body = white_ref[j, at : at + chans, :]
                top = jnp.where(row == 0, edge_ref[0, w : w + 1, lanes], body[:8])
                bottom = jnp.where(row == 7, edge_ref[1, w : w + 1, lanes], body[chans - 8 :])
                body = jnp.concatenate([top, body[8 : chans - 8], bottom], axis=0)
                held[pl.ds(half * windows + w, tile, stride=pitch), :] = body.T
        for f in range(tile):
            out_ref[block * tile + f] = held[f * pitch : f * pitch + 2 * windows, :].astype(BF16)


def turn(white, edge, chans, first, tiles):
    _, windows, width = edge.shape
    return call(
        functools.partial(turn_kernel, first),
        (white, edge),
        [VMEM, VMEM],
        [((tiles * LANES, 2 * windows, chans), BF16)],
        [pltpu.VMEM((LANES * (2 * windows + 8), chans), F32)],
        16,
        "turn",
    )[0]


def add_parts_kernel(keep_ref, came_ref, *outs):
    rows = outs[0].shape[0]
    for p, out in enumerate(outs):
        out[...] = keep_ref[p * rows : (p + 1) * rows] + came_ref[p * rows : (p + 1) * rows]


def add_parts(keep, came, after):
    rows, windows, width = keep.shape
    shape = (rows // 4, windows, width)
    return call(add_parts_kernel, (keep, came), [VMEM] * 2, [(shape, BF16)] * 4, [], 8, "add_parts", after)


def own_first_kernel(a_ref, b_ref, c_ref, d_ref, *refs):
    nexts, outs = refs[:3], refs[3:]
    rows = a_ref.shape[0]
    own = a_ref[...] + b_ref[...] + c_ref[...] + d_ref[...]
    for ref, out in zip(nexts, outs):
        out[:rows] = own
        out[rows:] = ref[...]


def own_first(pieces, nexts, after):
    rows, windows, width = pieces[0].shape
    return call(
        own_first_kernel,
        (*pieces, *nexts),
        [VMEM] * 7,
        [((2 * rows, windows, width), BF16)] * 3,
        [],
        8,
        "own_first",
        after,
    )


def part_kernel(sent_ref, b_ref, c_ref, d_ref, piece_ref, mine_ref, own_ref):
    rows = piece_ref.shape[0]
    for p, ref in enumerate((sent_ref, b_ref, c_ref, d_ref)):
        mine_ref[p * rows : (p + 1) * rows] = ref[:rows]
    own_ref[...] = piece_ref[...] + b_ref[rows:] + c_ref[rows:] + d_ref[rows:]


def part(sent, came, piece):
    rows, windows, width = piece.shape
    outs = [((4 * rows, windows, width), BF16), (piece.shape, BF16)]
    return call(part_kernel, (sent, *came, piece), [VMEM] * 5, outs, [], 8, "part")


def add_pair_kernel(keep_ref, *refs):
    out, rows = refs[-1], refs[0].shape[0]
    for k, ref in enumerate(refs[:-1]):
        at = slice(k * rows, (k + 1) * rows)
        out[at] = (keep_ref[at].astype(F32) + ref[...].astype(F32)).astype(BF16)


def add_pair(keep, came, after):
    ins = (keep, *came)
    return call(add_pair_kernel, ins, [VMEM] * len(ins), [(keep.shape, BF16)], [], 8, "add_pair", after)[0]


def bins_kernel(rows_ref, low_ref, high_ref, st, vt):
    rows, windows, width = rows_ref.shape
    held_freqs, depth, chans = low_ref.shape
    freqs = width // 2
    tile = LANES
    group = tile // depth
    for g in range(rows // group):
        pieces = []
        for s in range(g * group, (g + 1) * group):
            v = rows_ref[s].astype(F32)
            pieces += [v[:, :freqs], v[:, freqs:]]
        stack = jnp.concatenate(pieces, axis=0)
        for j in range(freqs // tile):
            t = stack[:, j * tile : (j + 1) * tile].T
            for i in range(group):
                moved = t if i == 0 else pltpu.roll(t, tile - i * depth, 1)
                vt[pl.ds(j * tile * rows + g * group + i, tile, stride=rows), :] = moved

    unroll = 128
    for which, ref in enumerate((low_ref, high_ref)):

        def step(i, carry):
            for k in range(unroll):
                f = i * unroll + k
                at = pl.multiple_of((which * held_freqs + f) * rows, 8)
                lhs = vt[pl.ds(at, rows), 0:depth].astype(BF16)
                x = ref[f]
                crossed = jnp.concatenate([x[windows:], -x[:windows]], axis=0)
                sums = jnp.dot(lhs, jnp.concatenate([x, crossed], axis=1), preferred_element_type=F32)
                st[0, pl.ds(at, rows), :] = sums[:, :chans]
                st[1, pl.ds(at, rows), :] = sums[:, chans:]
            return carry

        lax.fori_loop(0, held_freqs // unroll, step, 0)


def bins(rows, turned, after):
    count, windows, width = rows.shape
    held = width // 2 * count
    return call(
        bins_kernel,
        (rows, *turned),
        [VMEM] * 3,
        [((2, held, turned[0].shape[-1]), F32)],
        [pltpu.VMEM((held, LANES), F32)],
        8,
        "bins",
        after,
    )[0]


def lags_kernel(parts, st, cos_ref, sin_ref, *outs):
    rows = outs[0].shape[0]
    chans = st.shape[-1]
    freqs = st.shape[1] // rows
    me = lax.axis_index("win")
    share = chans // parts
    half = sin_ref.shape[0]
    last_row = lax.broadcasted_iota(jnp.int32, (8, 1), 0) == 7

    def transform(p, carry):
        real, imag = [
            jnp.concatenate([st[i, pl.ds(2 * p + k, freqs, stride=rows), :].astype(BF16) for k in (0, 1)], axis=1)
            for i in (0, 1)
        ]
        even = jnp.dot(cos_ref[...], real, preferred_element_type=F32)
        odd = jnp.dot(sin_ref[...], imag, preferred_element_type=F32)
        tail = odd[half - 8 :] + jnp.where(last_row, even[half : half + 1], 0.0)
        out = jnp.concatenate([even[:half], odd[: half - 8], tail], axis=0)
        for k in range(2):
            flat = out[:, k * chans : (k + 1) * chans].T.astype(BF16)
            for b in range(parts):
                value = flat[b * share : (b + 1) * share, :]
                for slot, to in enumerate(outs):

                    @pl.when(b ^ me == slot)
                    def _():
                        to[2 * p + k] = value

        return carry

    lax.fori_loop(0, rows // 2, transform, 0)


def lags(parts, rows, sums, tables, after):
    chans = sums.shape[-1]
    shape = (rows, chans // parts, LAGS)
    return call(
        functools.partial(lags_kernel, parts),
        (sums, *tables),
        [VMEM] * 3,
        [(shape, BF16)] * parts,
        [],
        8,
        "lags",
        after,
    )


def unfold_kernel(blocks, pairs, *refs):
    ins, mix_ref, earlier, (out_ref, held) = refs[: 3 * pairs], refs[3 * pairs], refs[3 * pairs + 1 : -2], refs[-2:]
    rows, chans, lags = ins[0].shape
    per_chunk = pairs * rows
    pitch = per_chunk + 8
    for pair in range(pairs):
        total = jnp.zeros((rows * chans, lags), F32)
        stay, near, far = [ref[...].reshape(rows * chans, lags) for ref in ins[3 * pair : 3 * pair + 3]]
        near = (stay.astype(F32) + near.astype(F32)).astype(BF16)
        for flat in (near, far):
            total = total + jnp.dot(flat, mix_ref[...], preferred_element_type=F32)
        for r in range(rows):
            at = source_at(blocks, pair * rows + r, per_chunk)
            for j in range(lags // LANES):
                lanes = slice(j * LANES, (j + 1) * LANES)
                held[j, pl.ds(at, chans, stride=pitch), :] = total[r * chans : (r + 1) * chans, lanes]
    first = out_ref.shape[1] - per_chunk
    for c in range(chans):
        if earlier:
            out_ref[c, :first, :] = earlier[0][c]
        for j in range(lags // LANES):
            lanes = slice(j * LANES, (j + 1) * LANES)
            out_ref[c, first:, lanes] = held[j, c * pitch : c * pitch + per_chunk, :].astype(BF16)


def unfold(blocks, ins, mix, earlier):
    rows, chans, lags = ins[0].shape
    per_chunk = len(ins) // 3 * rows
    return call(
        functools.partial(unfold_kernel, blocks, len(ins) // 3),
        (*ins, mix, *earlier),
        [VMEM] * (len(ins) + 1 + len(earlier)),
        [((chans, per_chunk * (1 + len(earlier)), lags), BF16)],
        [pltpu.VMEM((lags // LANES, chans * (per_chunk + 8), LANES), F32)],
        16,
        "unfold",
    )[0]


def meet_x(keep, send, after):
    return add_parts(keep, lax.ppermute(send, "chan", xor_pairs(8, 1)), after)


def over_z(arrays):
    return [lax.ppermute(array, "chan", xor_pairs(8, 2 * p)) for p, array in zip((1, 2, 3), arrays)]


def spread(blocks, picks, turned):
    if blocks != 8:
        return [lax.psum(pick, "chan") for pick in picks]
    pieces_a = meet_x(picks[0], picks[1], turned[:1])
    pieces_b = meet_x(picks[2], picks[3], ())
    sent = own_first([pieces_a[0]] + over_z(pieces_a[1:]), pieces_b[1:], turned[1:])
    mine_a, own_b = part(sent[0], over_z(sent), pieces_b[0])
    theirs_a = lax.ppermute(mine_a, "chan", xor_pairs(8, 1))
    mine_b = jnp.concatenate([own_b] + over_z([own_b] * 3), axis=0)
    return mine_a, theirs_a, mine_b, lax.ppermute(mine_b, "chan", xor_pairs(8, 1))


def lag_tables(freqs, windows):
    half = LAGS // 2
    f = np.arange(freqs)[None, :]
    scale = np.where(f == 0, 1.0, 2.0) * 0.25 / math.sqrt(freqs * windows)
    u = np.arange(half + 16)[:, None]
    cos = np.where(u <= half, scale * np.cos(math.pi * (f * u % (2 * freqs)) / freqs), 0.0)
    u = np.arange(1, half + 1)[:, None]
    sin = -scale * np.sin(math.pi * (f * u % (2 * freqs)) / freqs) * np.where(u == half, -1.0, 1.0)
    return jnp.asarray(cos.astype(ml_dtypes.bfloat16)), jnp.asarray(sin.astype(ml_dtypes.bfloat16))


def lag_mix():
    half = LAGS // 2
    mix = np.zeros((LAGS, LAGS))
    u = np.arange(half)
    mix[u, half + u] = 1
    u = np.arange(1, half)
    mix[u, half - u] = 1
    mix[half - 1 + u, half + u] = 1
    mix[half - 1 + u, half - u] = -1
    mix[LAGS - 1, 0] = 1
    return jnp.asarray(mix.astype(ml_dtypes.bfloat16))


def on_device(blocks, parts, spectra, valid, sources):
    windows, chans, width = spectra.shape
    freqs = width // 2
    forward = [(i, (i + 1) % blocks) for i in range(blocks)]
    backward = [(b, a) for a, b in forward]
    low = lax.ppermute(spectra[:, chans - 1 :, :], "chan", forward)
    high = lax.ppermute(spectra[:, :1, :], "chan", backward)
    white, band, part, raw = whiten(spectra)
    *picks, edge = edges(blocks, chans, valid, sources, low, high, white, band, part, raw)
    tables = lag_tables(freqs, windows)
    mix = lag_mix()
    tiles = freqs // LANES // 2
    turned = [turn(white, edge, chans, i * tiles, tiles) for i in range(2)]
    mine_a, theirs_a, mine_b, theirs_b = spread(blocks, picks, turned)

    def near(send):
        return lax.ppermute(send, "win", xor_pairs(parts, 1))

    def far(leave):
        return lax.ppermute(leave, "win", xor_pairs(parts, 2))

    pairs, cames, waiting = [], [], []

    def send_far(after):
        leave, came = waiting.pop()
        cames.append(far(add_pair(leave, came, after)))

    for i, rows in enumerate((mine_a, theirs_a, mine_b, theirs_b)):
        sums = bins(rows, turned, ())
        after = [mine_b, theirs_a] if i == 0 else cames[i - 2 : i - 1] if i > 1 else []
        stay, send_stay, leave, send_leave = lags(parts, rows.shape[0], sums, tables, after)
        half = rows.shape[0] // 2
        waiting.append((leave, [near(send_leave[:half]), near(send_leave[half:])]))
        send_far(cames[2:3])
        pairs += [(stay, near(send_stay))]
    pairs = [array for (stay, came), far_came in zip(pairs, cames) for array in (stay, came, far_came)]
    first = unfold(blocks, pairs[:6], mix, ())
    return unfold(blocks, pairs[6:], mix, (first,))


def solution(mesh):
    return jax.shard_map(
        functools.partial(on_device, mesh.shape["chan"], mesh.shape["win"]),
        mesh=mesh,
        in_specs=(P("win", "chan", None), P("win"), P()),
        out_specs=P(("chan", "win"), None, None),
        check_vma=False,
    )
```

```python
import functools
import math

import jax
import jax.numpy as jnp
import ml_dtypes
import numpy as np
from jax import lax
from jax.experimental import pallas as pl
from jax.experimental.pallas import tpu as pltpu
from jax.sharding import PartitionSpec as P

LAGS = 512
SMOOTH = 21
EPSILON = 1e-06
CHUNKS = 2
LANES = 128
AFTER = {
    "own_first": ("turned0", "turned1"),
    "lags2": ("far0",),
    "lags3": ("far1", "sums2", "theirs_b"),
    "lags1": ("other1",),
    "end0": ("far1",),
    "bins1": ("other1",),
    "bins2": ("leave1",),
    "lags0": ("mine_a",),
    "part": ("mine_a", "turned0"),
    "gather": ("sums0",),
    "meet_a": ("turned0",),
}
F32 = jnp.float32
BF16 = jnp.bfloat16
MIB = 1024 * 1024
SMEM = pl.BlockSpec(memory_space=pltpu.SMEM)
VMEM = pl.BlockSpec(memory_space=pltpu.VMEM)
ANY = pl.BlockSpec(memory_space=pl.ANY)
HBM = pl.BlockSpec(memory_space=pltpu.HBM)


def call(kernel, ins, in_specs, outs, scratch, limit, name, after=()):
    count = len(ins)

    def body(*refs):
        kernel(*refs[:count], *refs[count + len(after) :])

    return pl.pallas_call(
        body,
        in_specs=[*in_specs] + [ANY] * len(after),
        out_specs=[VMEM] * len(outs),
        out_shape=[jax.ShapeDtypeStruct(shape, dtype) for shape, dtype in outs],
        scratch_shapes=scratch,
        compiler_params=pltpu.CompilerParams(vmem_limit_bytes=limit * MIB),
        cost_estimate=pl.CostEstimate(flops=0, bytes_accessed=16, transcendentals=0),
        name=name,
    )(*ins, *after)


def xor_pairs(count, mask):
    return [(i, i ^ mask) for i in range(count)]


def place(blocks):
    if blocks != 8:
        return 0, 0
    at = lax.axis_index("chan")
    return at % 2, at // 2


def source_at(blocks, r, per_chunk):
    x, z = place(blocks)
    quarter = per_chunk // 8
    chunk, r = divmod(r, per_chunk)
    half, r = divmod(r, 4 * quarter)
    part, i = divmod(r, quarter)
    return chunk * per_chunk + (x ^ half) * 4 * quarter + (z ^ part) * quarter + i


def amplitude(values):
    freqs = values.shape[-1] // 2
    real, imag = values[:, :freqs], values[:, freqs:]
    square = real * real + imag * imag
    return square * lax.rsqrt(jnp.maximum(square, 1e-36))


def bin_share(freqs):
    f = lax.broadcasted_iota(jnp.int32, (1, freqs), 1)
    entries = jnp.minimum(f, SMOOTH) + jnp.minimum(freqs - 1 - f, SMOOTH) + 1
    return 1.0 / (3.0 * entries.astype(F32))


def inverse_divisor(triple, band, share):
    divisor = jnp.dot(triple, band, preferred_element_type=F32) * share + EPSILON
    near = pl.reciprocal(divisor, approx=True)
    return near * (2.0 - divisor * near)


def whiten_kernel(spec_ref, white_ref, band, part_ref, raw_ref, buf, tri, inv, sems):
    windows, chans, width = buf.shape
    freqs = width // 2
    pitch = chans + 8
    together = tri.shape[0] // chans

    def fetch(w):
        return pltpu.make_async_copy(spec_ref.at[w], buf.at[w], sems.at[w])

    for w in range(windows):
        fetch(w).start()
    row = lax.broadcasted_iota(jnp.int32, (freqs, freqs), 0)
    col = lax.broadcasted_iota(jnp.int32, (freqs, freqs), 1)
    band[...] = jnp.where(jnp.abs(row - col) <= SMOOTH, 1.0, 0.0).astype(BF16)
    share = bin_share(freqs)

    def some(i, carry):
        for k in range(together):
            w = i * together + k
            fetch(w).wait()
            values = buf[w].astype(F32)
            magnitude = amplitude(values)
            triple = pltpu.roll(magnitude, 1, 0) + magnitude + pltpu.roll(magnitude, chans - 1, 0)
            tri[k * chans : (k + 1) * chans, :] = triple.astype(BF16)
            part_ref[0, pl.ds(w, 1), :] = magnitude[0:1] + magnitude[1:2]
            part_ref[1, pl.ds(w, 1), :] = magnitude[chans - 2 : chans - 1] + magnitude[chans - 1 :]
            raw_ref[0, pl.ds(w, 1), :] = values[0:1]
            raw_ref[1, pl.ds(w, 1), :] = values[chans - 1 :]
        inv[...] = inverse_divisor(tri[...], band[...], share)
        for k in range(together):
            w = i * together + k
            at = pl.multiple_of(w * pitch, 8)
            for j in range(width // LANES):
                values = buf[w, :, j * LANES : (j + 1) * LANES].astype(F32)
                first = j * LANES % freqs
                factor = inv[k * chans : (k + 1) * chans, first : first + LANES]
                white_ref[j, pl.ds(at, chans), :] = values * factor
        return carry

    lax.fori_loop(0, windows // together, some, 0)


def whiten(spectra):
    windows, chans, width = spectra.shape
    freqs = width // 2
    together = 4
    return call(
        whiten_kernel,
        (spectra,),
        [HBM],
        [
            ((width // LANES, windows * (chans + 8), LANES), F32),
            ((freqs, freqs), BF16),
            ((2, windows, freqs), F32),
            ((2, windows, width), F32),
        ],
        [
            pltpu.VMEM(spectra.shape, BF16),
            pltpu.VMEM((together * chans, freqs), BF16),
            pltpu.VMEM((together * chans, freqs), F32),
            pltpu.SemaphoreType.DMA((windows,)),
        ],
        28,
        "whiten",
    )


def edges_kernel(blocks, chans, src_ref, valid_ref, low_ref, high_ref, white_ref, band, part_ref, raw_ref, *outs):
    picks, edge_ref = outs[:-1], outs[-1]
    windows, width = raw_ref.shape[1:]
    freqs = width // 2
    sources = src_ref.shape[0]
    pitch = chans + 8
    share = bin_share(freqs)
    row = lax.broadcasted_iota(jnp.int32, (windows, 1), 0)
    valid = jnp.zeros((windows, 1), F32)
    for w in range(windows):
        valid = valid + jnp.where(row == w, valid_ref[w].astype(F32), 0.0)
    for k, ref in enumerate((low_ref, high_ref)):
        beside = jnp.concatenate([ref[w] for w in range(windows)], axis=0).astype(F32)
        triple = (part_ref[k] + amplitude(beside)).astype(BF16)
        inverse = inverse_divisor(triple, band[...], share)
        edge_ref[k] = raw_ref[k] * jnp.concatenate([inverse, inverse], axis=1)
    offset = lax.axis_index("chan") * chans
    rows = picks[0].shape[0]
    for r in range(sources):
        at = src_ref[source_at(blocks, r, sources // CHUNKS)] - offset
        inner = valid * ((at > 0) & (at < chans - 1)).astype(F32)
        first = valid * (at == 0).astype(F32)
        last = valid * (at == chans - 1).astype(F32)
        row_at = jnp.clip(at, 0, chans - 1)
        for j in range(width // LANES):
            lanes = slice(j * LANES, (j + 1) * LANES)
            value = inner * white_ref[j, pl.ds(row_at, windows, stride=pitch), :]
            value = value + first * edge_ref[0, :, lanes] + last * edge_ref[1, :, lanes]
            picks[r // rows][r % rows, :, lanes] = value.astype(BF16)


def edges(blocks, chans, valid, sources, low, high, white, band, part, raw):
    _, windows, width = raw.shape
    rows = sources.shape[0] // CHUNKS // 2
    return call(
        functools.partial(edges_kernel, blocks, chans),
        (sources, valid, low, high, white, band, part, raw),
        [SMEM, SMEM] + [VMEM] * 6,
        [((rows, windows, width), BF16)] * (2 * CHUNKS) + [(raw.shape, F32)],
        [],
        8,
        "edges",
    )


def halve_kernel(white_ref, edge_ref, keep_ref, send_ref):
    windows, chans, width = keep_ref.shape
    share = chans // 2
    blocks = white_ref.shape[1] // windows // share
    pitch = white_ref.shape[1] // windows
    me = lax.axis_index("win")
    row = lax.broadcasted_iota(jnp.int32, (8, LANES), 0)

    for w in range(windows):
        for out, first in ((keep_ref, me), (send_ref, me ^ 1)):
            for q in range(2):
                block = first ^ (2 * q)
                at = pl.multiple_of(w * pitch + block * share, 8)
                for j in range(width // LANES):
                    lanes = slice(j * LANES, (j + 1) * LANES)
                    body = white_ref[j, pl.ds(at, share), :]
                    top = jnp.where((row == 0) & (block == 0), edge_ref[0, w : w + 1, lanes], body[:8])
                    low = jnp.where((row == 7) & (block == blocks - 1), edge_ref[1, w : w + 1, lanes], body[share - 8 :])
                    body = jnp.concatenate([top, body[8 : share - 8], low], axis=0)
                    out[w, q * share : (q + 1) * share, lanes] = body.astype(BF16)


def halve(parts, white, edge, chans):
    _, windows, width = edge.shape
    shape = (windows, 2 * chans // parts, width)
    return call(halve_kernel, (white, edge), [VMEM] * 2, [(shape, BF16)] * 2, [], 8, "halve")


def turn_kernel(white_ref, out_ref, held):
    windows, chans, width = white_ref.shape
    tile = LANES
    pitch = 2 * windows + 8

    def block(b, carry):
        for w in range(windows):
            for half in range(2):
                at = pl.multiple_of(half * (width // 2) + b * tile, tile)
                body = white_ref[w, :, pl.ds(at, tile)].astype(F32)
                held[pl.ds(half * windows + w, tile, stride=pitch), :] = jnp.concatenate([body, body], axis=0).T
        for f in range(tile):
            out_ref[b * tile + f] = held[f * pitch : f * pitch + 2 * windows, :].astype(BF16)
        return carry

    lax.fori_loop(0, width // 2 // tile, block, 0)


def turn(white):
    windows, chans, width = white.shape
    return call(
        turn_kernel,
        (white,),
        [VMEM],
        [((width // 2, 2 * windows, 2 * chans), BF16)],
        [pltpu.VMEM((LANES * (2 * windows + 8), LANES), F32)],
        8,
        "turn",
    )[0]


def add_parts_kernel(keep_ref, came_ref, *outs):
    rows = outs[0].shape[0]
    for p, out in enumerate(outs):
        out[...] = keep_ref[p * rows : (p + 1) * rows] + came_ref[p * rows : (p + 1) * rows]


def add_parts(keep, came, after):
    rows, windows, width = keep.shape
    shape = (rows // 4, windows, width)
    return call(add_parts_kernel, (keep, came), [VMEM] * 2, [(shape, BF16)] * 4, [], 8, "add_parts", after)


def own_first_kernel(a_ref, b_ref, c_ref, d_ref, *refs):
    nexts, outs = refs[:3], refs[3:]
    rows = a_ref.shape[0]
    own = a_ref[...] + b_ref[...] + c_ref[...] + d_ref[...]
    for ref, out in zip(nexts, outs):
        out[:rows] = own
        out[rows:] = ref[...]


def own_first(pieces, nexts, after):
    rows, windows, width = pieces[0].shape
    return call(
        own_first_kernel,
        (*pieces, *nexts),
        [VMEM] * 7,
        [((2 * rows, windows, width), BF16)] * 3,
        [],
        8,
        "own_first",
        after,
    )


def gather_kernel(sent_ref, b_ref, c_ref, d_ref, mine_ref):
    rows = mine_ref.shape[0] // 4
    for p, ref in enumerate((sent_ref, b_ref, c_ref, d_ref)):
        mine_ref[p * rows : (p + 1) * rows] = ref[:rows]


def gather(parts_by_z, rows, after=()):
    shape = (4 * rows, *parts_by_z[0].shape[1:])
    return call(gather_kernel, parts_by_z, [VMEM] * 4, [(shape, BF16)], [], 8, "gather", after)[0]


def part_kernel(b_ref, c_ref, d_ref, piece_ref, own_ref):
    rows = piece_ref.shape[0]
    own_ref[...] = piece_ref[...] + b_ref[rows:] + c_ref[rows:] + d_ref[rows:]


def part(came, piece, after=()):
    return call(part_kernel, (*came, piece), [VMEM] * 4, [(piece.shape, BF16)], [], 8, "part", after)[0]


def bins_kernel(own_ref, other_ref, low_ref, high_ref, st, vt):
    rows, windows, width = own_ref.shape
    depth, lanes = low_ref.shape[1:]
    freqs = width // 2
    tile = LANES
    pairs = rows // 2
    for p in range(pairs):
        whole, crossed = [], []
        for s in (2 * p, 2 * p + 1):
            for ref in (own_ref, other_ref):
                v = ref[s].astype(F32)
                whole += [v[:, :freqs], v[:, freqs:]]
                crossed += [-v[:, freqs:], v[:, :freqs]]
        for k, pieces in enumerate((whole, crossed)):
            stack = jnp.concatenate(pieces, axis=0)
            for j in range(freqs // tile):
                turned = stack[:, j * tile : (j + 1) * tile].T
                at = j * tile * 2 * rows + k * pairs + p
                vt[pl.ds(at, tile, stride=2 * rows), :] = turned
                vt[pl.ds(at + rows, tile, stride=2 * rows), :] = pltpu.roll(turned, tile // 2, 1)

    first = lax.broadcasted_iota(jnp.int32, (rows, lanes), 1) < lanes // 2
    unroll = 256

    def step(i, carry):
        for k in range(unroll):
            f = i * unroll + k
            lhs = vt[pl.ds(pl.multiple_of(f * 2 * rows, 8), 2 * rows), : 2 * depth].astype(BF16)
            x = jnp.concatenate([low_ref[f], high_ref[f]], axis=0)
            sums = jnp.dot(lhs, x, preferred_element_type=F32)
            st[pl.ds(pl.multiple_of(f * rows, 8), rows), :] = jnp.where(first, sums[:rows], sums[rows:])
        return carry

    lax.fori_loop(0, freqs // unroll, step, 0)


def bins(own, other, turned, after):
    count, windows, width = own.shape
    held = width // 2 * count
    return call(
        bins_kernel,
        (own, other, *turned),
        [VMEM] * 4,
        [((held, LANES), F32)],
        [pltpu.VMEM((2 * held, LANES), F32)],
        10,
        "bins",
        after,
    )[0]


def lags_kernel(st, cos_ref, sin_ref, stay_ref, leave_ref):
    rows, share = stay_ref.shape[:2]
    pairs = rows // 2
    freqs = st.shape[0] // rows
    half = sin_ref.shape[0]
    last_row = lax.broadcasted_iota(jnp.int32, (8, 1), 0) == 7
    for q in range(pairs // 2):
        real, imag = [
            jnp.concatenate(
                [st[pl.ds(i * pairs + 2 * q + k, freqs, stride=rows), :].astype(BF16) for k in (0, 1)], axis=1
            )
            for i in (0, 1)
        ]
        even = jnp.dot(cos_ref[...], real, preferred_element_type=F32)
        odd = jnp.dot(sin_ref[...], imag, preferred_element_type=F32)
        tail = odd[half - 8 :] + jnp.where(last_row, even[half : half + 1], 0.0)
        out = jnp.concatenate([even[:half], odd[: half - 8], tail], axis=0)
        for k in range(2):
            flat = out[:, k * LANES : (k + 1) * LANES].T.astype(BF16)
            for s in range(2):
                at = 2 * share * s
                stay_ref[4 * q + 2 * k + s] = flat[at : at + share]
                leave_ref[4 * q + 2 * k + s] = flat[at + share : at + 2 * share]


def lags(share, rows, sums, tables, after):
    shape = (rows, share, LAGS)
    return call(lags_kernel, (sums, *tables), [VMEM] * 3, [(shape, BF16)] * 2, [], 10, "lags", after)


def unfold_kernel(blocks, pairs, *refs):
    ins, mix_ref, earlier, (out_ref, held) = refs[: 2 * pairs], refs[2 * pairs], refs[2 * pairs + 1 : -2], refs[-2:]
    rows, chans, lags = ins[0].shape
    per_chunk = pairs * rows
    pitch = per_chunk + 8
    for pair in range(pairs):
        total = jnp.zeros((rows * chans, lags), F32)
        for ref in ins[2 * pair : 2 * pair + 2]:
            flat = ref[...].reshape(rows * chans, lags)
            total = total + jnp.dot(flat, mix_ref[...], preferred_element_type=F32)
        for r in range(rows):
            at = source_at(blocks, pair * rows + r, per_chunk)
            for j in range(lags // LANES):
                lanes = slice(j * LANES, (j + 1) * LANES)
                held[j, pl.ds(at, chans, stride=pitch), :] = total[r * chans : (r + 1) * chans, lanes]
    first = out_ref.shape[1] - per_chunk
    for c in range(chans):
        if earlier:
            out_ref[c, :first, :] = earlier[0][c]
        for j in range(lags // LANES):
            lanes = slice(j * LANES, (j + 1) * LANES)
            out_ref[c, first:, lanes] = held[j, c * pitch : c * pitch + per_chunk, :].astype(BF16)


def unfold(blocks, ins, mix, earlier, after):
    rows, chans, lags = ins[0].shape
    per_chunk = len(ins) // 2 * rows
    return call(
        functools.partial(unfold_kernel, blocks, len(ins) // 2),
        (*ins, mix, *earlier),
        [VMEM] * (len(ins) + 1 + len(earlier)),
        [((chans, per_chunk * (1 + len(earlier)), lags), BF16)],
        [pltpu.VMEM((lags // LANES, chans * (per_chunk + 8), LANES), F32)],
        16,
        "unfold",
        after,
    )[0]


def meet_x(keep, send, after):
    return add_parts(keep, lax.ppermute(send, "chan", xor_pairs(8, 1)), after)


def over_z(arrays):
    return [lax.ppermute(array, "chan", xor_pairs(8, 2 * p)) for p, array in zip((1, 2, 3), arrays)]


def over_x(array):
    return lax.ppermute(array, "chan", xor_pairs(8, 1))


def lag_tables(freqs, windows):
    half = LAGS // 2
    f = np.arange(freqs)[None, :]
    scale = np.where(f == 0, 1.0, 2.0) * 0.25 / math.sqrt(freqs * windows)
    u = np.arange(half + 16)[:, None]
    cos = np.where(u <= half, scale * np.cos(math.pi * (f * u % (2 * freqs)) / freqs), 0.0)
    u = np.arange(1, half + 1)[:, None]
    sin = -scale * np.sin(math.pi * (f * u % (2 * freqs)) / freqs) * np.where(u == half, -1.0, 1.0)
    return jnp.asarray(cos.astype(ml_dtypes.bfloat16)), jnp.asarray(sin.astype(ml_dtypes.bfloat16))


def lag_mix():
    half = LAGS // 2
    mix = np.zeros((LAGS, LAGS))
    u = np.arange(half)
    mix[u, half + u] = 1
    u = np.arange(1, half)
    mix[u, half - u] = 1
    mix[half - 1 + u, half + u] = 1
    mix[half - 1 + u, half - u] = -1
    mix[LAGS - 1, 0] = 1
    return jnp.asarray(mix.astype(ml_dtypes.bfloat16))


def on_device(blocks, parts, spectra, valid, sources):
    windows, chans, width = spectra.shape
    freqs = width // 2
    forward = [(i, (i + 1) % blocks) for i in range(blocks)]
    backward = [(b, a) for a, b in forward]
    low = lax.ppermute(spectra[:, chans - 1 :, :], "chan", forward)
    high = lax.ppermute(spectra[:, :1, :], "chan", backward)
    white, band, edge_sums, raw = whiten(spectra)
    *picks, edge = edges(blocks, chans, valid, sources, low, high, white, band, edge_sums, raw)
    tables = lag_tables(freqs, windows)
    mix = lag_mix()

    def near(array):
        return lax.ppermute(array, "win", xor_pairs(parts, 1))

    def far(array):
        return lax.ppermute(array, "win", xor_pairs(parts, 2))

    keep, send = halve(parts, white, edge, chans)
    turned = [turn(keep), turn(near(send))]
    made = {"turned0": turned[0], "turned1": turned[1]}
    ends = []

    def after(name):
        return [made[key] for key in AFTER.get(name, ()) if key in made]

    def swap(name, rows):
        made[name] = rows
        made[name + "_near"] = near(rows)

    def put(i, name):
        made[f"sums{i}"] = bins(made[name], made[name + "_near"], turned, after(f"bins{i}"))

    def transform(i):
        sums = made[f"sums{i}"]
        stay, leave = lags(chans // parts, sums.shape[0] // freqs, sums, tables, after(f"lags{i}"))
        made[f"leave{i}"] = leave
        made[f"far{i}"] = far(leave)
        ends.extend([stay, made[f"far{i}"]])

    def end(chunk, earlier):
        return unfold(blocks, ends[4 * chunk : 4 * chunk + 4], mix, earlier, after(f"end{chunk}"))

    if blocks == 8:
        pieces_a = meet_x(picks[0], picks[1], after("meet_a"))
        pieces_b = meet_x(picks[2], picks[3], ())
        sent = own_first([pieces_a[0]] + over_z(pieces_a[1:]), pieces_b[1:], after("own_first"))
        came = over_z(sent)
        rows = pieces_b[0].shape[0]
        swap("mine_a", gather((sent[0], *came), rows))
        swap("theirs_a", over_x(made["mine_a"]))
        made["own_b"] = own_b = part(came, pieces_b[0], after("part"))
        others = over_z([own_b] * 3)
        made["other0"], made["other1"], made["other2"] = others
        put(0, "mine_a")
        transform(0)
        swap("mine_b", gather((own_b, *others), rows, after("gather")))
        swap("theirs_b", over_x(made["mine_b"]))
    else:
        for name, pick in zip(("mine_a", "theirs_a", "mine_b", "theirs_b"), picks):
            swap(name, lax.psum(pick, "chan"))
        put(0, "mine_a")
        transform(0)
    for i, name in ((1, "theirs_a"), (2, "mine_b"), (3, "theirs_b")):
        put(i, name)
        transform(i)
    return end(1, (end(0, ()),))


def solution(mesh):
    return jax.shard_map(
        functools.partial(on_device, mesh.shape["chan"], mesh.shape["win"]),
        mesh=mesh,
        in_specs=(P("win", "chan", None), P("win"), P()),
        out_specs=P(("chan", "win"), None, None),
        check_vma=False,
    )
```

```python
import functools
import math

import jax
import jax.numpy as jnp
import ml_dtypes
import numpy as np
from jax import lax
from jax.experimental import pallas as pl
from jax.experimental.pallas import tpu as pltpu
from jax.sharding import PartitionSpec as P

LAGS = 512
SMOOTH = 21
EPSILON = 1e-06
CHUNKS = 2
LANES = 128
AFTER = {
    "halve": ("pieces_a",),
    "own_first": ("turned0",),
    "gather_a": ("turned1",),
    "lags3": ("far2", "sums1"),
    "gather": ("leave0", "mine_a_near", "other0", "own_b", "theirs_a"),
    "bins3": ("leave1", "sums1", "sums2", "theirs_b", "theirs_b_near"),
    "lags1": ("far0", "other2"),
    "end0": ("leave1", "leave2", "sums1", "theirs_b"),
    "bins1": ("mine_b", "other0", "theirs_b"),
    "part": ("pieces_a",),
    "lags0": ("mine_a", "other0", "other1", "sums0", "turned1"),
    "lags2": ("leave0",),
}
F32 = jnp.float32
BF16 = jnp.bfloat16
MIB = 1024 * 1024
SMEM = pl.BlockSpec(memory_space=pltpu.SMEM)
VMEM = pl.BlockSpec(memory_space=pltpu.VMEM)
ANY = pl.BlockSpec(memory_space=pl.ANY)
HBM = pl.BlockSpec(memory_space=pltpu.HBM)


def call(kernel, ins, in_specs, outs, scratch, limit, name, after=(), aliases=None):
    count = len(ins)

    def body(*refs):
        kernel(*refs[:count], *refs[count + len(after) :])

    return pl.pallas_call(
        body,
        in_specs=[*in_specs] + [ANY] * len(after),
        out_specs=[VMEM] * len(outs),
        out_shape=[jax.ShapeDtypeStruct(shape, dtype) for shape, dtype in outs],
        scratch_shapes=scratch,
        input_output_aliases=aliases or {},
        compiler_params=pltpu.CompilerParams(vmem_limit_bytes=limit * MIB),
        cost_estimate=pl.CostEstimate(flops=0, bytes_accessed=16, transcendentals=0),
        name=name,
    )(*ins, *after)


def xor_pairs(count, mask):
    return [(i, i ^ mask) for i in range(count)]


def place(blocks):
    if blocks != 8:
        return 0, 0
    at = lax.axis_index("chan")
    return at % 2, at // 2


def source_at(blocks, r, per_chunk):
    x, z = place(blocks)
    quarter = per_chunk // 8
    chunk, r = divmod(r, per_chunk)
    half, r = divmod(r, 4 * quarter)
    part, i = divmod(r, quarter)
    return chunk * per_chunk + (x ^ half) * 4 * quarter + (z ^ part) * quarter + i


def source_row(blocks, r, count):
    per_chunk = count // CHUNKS
    return r // per_chunk * per_chunk + source_at(blocks, r % per_chunk, per_chunk)


def amplitude(values):
    freqs = values.shape[-1] // 2
    real, imag = values[:, :freqs], values[:, freqs:]
    square = real * real + imag * imag
    return square * lax.rsqrt(jnp.maximum(square, 1e-36))


def bin_share(freqs):
    f = lax.broadcasted_iota(jnp.int32, (1, freqs), 1)
    entries = jnp.minimum(f, SMOOTH) + jnp.minimum(freqs - 1 - f, SMOOTH) + 1
    return 1.0 / (3.0 * entries.astype(F32))


def inverse_divisor(triple, band, share):
    divisor = jnp.dot(triple, band, preferred_element_type=F32) * share + EPSILON
    near = pl.reciprocal(divisor, approx=True)
    return near * (2.0 - divisor * near)


def rim_kernel(spec_ref, first_ref, last_ref):
    windows, chans, _ = spec_ref.shape
    for w in range(windows):
        first_ref[w] = spec_ref[w, :16].astype(F32)[:1].astype(BF16)
        last_ref[w] = spec_ref[w, chans - 16 :].astype(F32)[15:].astype(BF16)


def rim(spectra):
    windows, _, width = spectra.shape
    return call(rim_kernel, (spectra,), [VMEM], [((windows, 1, width), BF16)] * 2, [], 8, "rim")


def whiten_kernel(spec_ref, white_ref, band, part_ref, raw_ref, buf, tri, inv, sems):
    windows, chans, width = buf.shape
    freqs = width // 2
    pitch = chans + 8
    together = tri.shape[0] // chans

    def fetch(w):
        return pltpu.make_async_copy(spec_ref.at[w], buf.at[w], sems.at[w])

    for w in range(windows):
        fetch(w).start()
    row = lax.broadcasted_iota(jnp.int32, (freqs, freqs), 0)
    col = lax.broadcasted_iota(jnp.int32, (freqs, freqs), 1)
    band[...] = jnp.where(jnp.abs(row - col) <= SMOOTH, 1.0, 0.0).astype(BF16)
    share = bin_share(freqs)

    def some(i, carry):
        for k in range(together):
            w = i * together + k
            fetch(w).wait()
            values = buf[w].astype(F32)
            magnitude = amplitude(values)
            triple = pltpu.roll(magnitude, 1, 0) + magnitude + pltpu.roll(magnitude, chans - 1, 0)
            tri[k * chans : (k + 1) * chans, :] = triple.astype(BF16)
            part_ref[0, pl.ds(w, 1), :] = magnitude[0:1] + magnitude[1:2]
            part_ref[1, pl.ds(w, 1), :] = magnitude[chans - 2 : chans - 1] + magnitude[chans - 1 :]
            raw_ref[0, pl.ds(w, 1), :] = values[0:1]
            raw_ref[1, pl.ds(w, 1), :] = values[chans - 1 :]
        inv[...] = inverse_divisor(tri[...], band[...], share)
        for k in range(together):
            w = i * together + k
            at = pl.multiple_of(w * pitch, 8)
            for j in range(width // LANES):
                values = buf[w, :, j * LANES : (j + 1) * LANES].astype(F32)
                first = j * LANES % freqs
                factor = inv[k * chans : (k + 1) * chans, first : first + LANES]
                white_ref[j, pl.ds(at, chans), :] = values * factor
        return carry

    lax.fori_loop(0, windows // together, some, 0)


def whiten(spectra):
    windows, chans, width = spectra.shape
    freqs = width // 2
    together = 4
    return call(
        whiten_kernel,
        (spectra,),
        [HBM],
        [
            ((width // LANES, windows * (chans + 8), LANES), F32),
            ((freqs, freqs), BF16),
            ((2, windows, freqs), F32),
            ((2, windows, width), F32),
        ],
        [
            pltpu.VMEM(spectra.shape, BF16),
            pltpu.VMEM((together * chans, freqs), BF16),
            pltpu.VMEM((together * chans, freqs), F32),
            pltpu.SemaphoreType.DMA((windows,)),
        ],
        28,
        "whiten",
    )


def edges_kernel(blocks, chans, src_ref, valid_ref, low_ref, high_ref, white_ref, band, part_ref, raw_ref, *outs):
    picks, edge_ref = outs[:-1], outs[-1]
    windows, width = raw_ref.shape[1:]
    freqs = width // 2
    sources = src_ref.shape[0]
    pitch = chans + 8
    share = bin_share(freqs)
    row = lax.broadcasted_iota(jnp.int32, (windows, 1), 0)
    valid = jnp.zeros((windows, 1), F32)
    for w in range(windows):
        valid = valid + jnp.where(row == w, valid_ref[w].astype(F32), 0.0)
    for k, ref in enumerate((low_ref, high_ref)):
        beside = jnp.concatenate([ref[w] for w in range(windows)], axis=0).astype(F32)
        triple = (part_ref[k] + amplitude(beside)).astype(BF16)
        inverse = inverse_divisor(triple, band[...], share)
        edge_ref[k] = raw_ref[k] * jnp.concatenate([inverse, inverse], axis=1)
    offset = lax.axis_index("chan") * chans
    rows = picks[0].shape[0]
    for r in range(sources):
        at = src_ref[source_at(blocks, r, sources // CHUNKS)] - offset
        inner = valid * ((at > 0) & (at < chans - 1)).astype(F32)
        first = valid * (at == 0).astype(F32)
        last = valid * (at == chans - 1).astype(F32)
        row_at = jnp.clip(at, 0, chans - 1)
        for j in range(width // LANES):
            lanes = slice(j * LANES, (j + 1) * LANES)
            value = inner * white_ref[j, pl.ds(row_at, windows, stride=pitch), :]
            value = value + first * edge_ref[0, :, lanes] + last * edge_ref[1, :, lanes]
            picks[r // rows][r % rows, :, lanes] = value.astype(BF16)


def edges(blocks, chans, valid, sources, low, high, white, band, part, raw):
    _, windows, width = raw.shape
    rows = sources.shape[0] // CHUNKS // 2
    return call(
        functools.partial(edges_kernel, blocks, chans),
        (sources, valid, low, high, white, band, part, raw),
        [SMEM, SMEM] + [VMEM] * 6,
        [((rows, windows, width), BF16)] * (2 * CHUNKS) + [(raw.shape, F32)],
        [],
        8,
        "edges",
    )


def halve_kernel(white_ref, edge_ref, keep_ref, send_ref):
    windows, chans, width = keep_ref.shape
    share = chans // 2
    blocks = white_ref.shape[1] // windows // share
    pitch = white_ref.shape[1] // windows
    me = lax.axis_index("win")
    row = lax.broadcasted_iota(jnp.int32, (8, LANES), 0)

    for w in range(windows):
        for out, first in ((keep_ref, me), (send_ref, me ^ 1)):
            for q in range(2):
                block = first ^ (2 * q)
                at = pl.multiple_of(w * pitch + block * share, 8)
                for j in range(width // LANES):
                    lanes = slice(j * LANES, (j + 1) * LANES)
                    body = white_ref[j, pl.ds(at, share), :]
                    top = jnp.where((row == 0) & (block == 0), edge_ref[0, w : w + 1, lanes], body[:8])
                    low = jnp.where((row == 7) & (block == blocks - 1), edge_ref[1, w : w + 1, lanes], body[share - 8 :])
                    body = jnp.concatenate([top, body[8 : share - 8], low], axis=0)
                    out[w, q * share : (q + 1) * share, lanes] = body.astype(BF16)


def halve(parts, white, edge, chans, after):
    _, windows, width = edge.shape
    shape = (windows, 2 * chans // parts, width)
    return call(halve_kernel, (white, edge), [VMEM] * 2, [(shape, BF16)] * 2, [], 8, "halve", after)


def turn_kernel(white_ref, out_ref, held):
    windows, chans, width = white_ref.shape
    tile = LANES
    pitch = 2 * windows + 8

    def block(b, carry):
        for w in range(windows):
            for half in range(2):
                at = pl.multiple_of(half * (width // 2) + b * tile, tile)
                body = white_ref[w, :, pl.ds(at, tile)].astype(F32)
                held[pl.ds(half * windows + w, tile, stride=pitch), :] = jnp.concatenate([body, body], axis=0).T
        for f in range(tile):
            out_ref[b * tile + f] = held[f * pitch : f * pitch + 2 * windows, :].astype(BF16)
        return carry

    lax.fori_loop(0, width // 2 // tile, block, 0)


def turn(white):
    windows, chans, width = white.shape
    return call(
        turn_kernel,
        (white,),
        [VMEM],
        [((width // 2, 2 * windows, 2 * chans), BF16)],
        [pltpu.VMEM((LANES * (2 * windows + 8), LANES), F32)],
        8,
        "turn",
    )[0]


def add_parts_kernel(keep_ref, came_ref, *outs):
    rows = outs[0].shape[0]
    for p, out in enumerate(outs):
        out[...] = keep_ref[p * rows : (p + 1) * rows] + came_ref[p * rows : (p + 1) * rows]


def add_parts(keep, came, after):
    rows, windows, width = keep.shape
    shape = (rows // 4, windows, width)
    return call(add_parts_kernel, (keep, came), [VMEM] * 2, [(shape, BF16)] * 4, [], 8, "add_parts", after)


def own_first_kernel(a_ref, b_ref, c_ref, d_ref, *refs):
    nexts, outs = refs[:3], refs[3:]
    rows = a_ref.shape[0]
    own = a_ref[...] + b_ref[...] + c_ref[...] + d_ref[...]
    for ref, out in zip(nexts, outs):
        out[:rows] = own
        out[rows:] = ref[...]


def own_first(pieces, nexts, after):
    rows, windows, width = pieces[0].shape
    return call(
        own_first_kernel,
        (*pieces, *nexts),
        [VMEM] * 7,
        [((2 * rows, windows, width), BF16)] * 3,
        [],
        8,
        "own_first",
        after,
    )


def gather_kernel(sent_ref, b_ref, c_ref, d_ref, mine_ref):
    rows = mine_ref.shape[0] // 4
    for p, ref in enumerate((sent_ref, b_ref, c_ref, d_ref)):
        mine_ref[p * rows : (p + 1) * rows] = ref[:rows]


def gather(parts_by_z, rows, after=()):
    shape = (4 * rows, *parts_by_z[0].shape[1:])
    return call(gather_kernel, parts_by_z, [VMEM] * 4, [(shape, BF16)], [], 8, "gather", after)[0]


def part_kernel(b_ref, c_ref, d_ref, piece_ref, own_ref):
    rows = piece_ref.shape[0]
    own_ref[...] = piece_ref[...] + b_ref[rows:] + c_ref[rows:] + d_ref[rows:]


def part(came, piece, after=()):
    return call(part_kernel, (*came, piece), [VMEM] * 4, [(piece.shape, BF16)], [], 8, "part", after)[0]


def bins_kernel(own_ref, other_ref, low_ref, high_ref, st, vt):
    rows, windows, width = own_ref.shape
    depth, lanes = low_ref.shape[1:]
    freqs = width // 2
    tile = LANES
    pairs = rows // 2
    for p in range(pairs):
        pieces = []
        for s in (2 * p, 2 * p + 1):
            for ref in (own_ref, other_ref):
                v = ref[s].astype(F32)
                pieces += [v[:, :freqs], v[:, freqs:]]
        stack = jnp.concatenate(pieces, axis=0)
        for j in range(freqs // tile):
            turned = stack[:, j * tile : (j + 1) * tile].T
            at = j * tile * rows + p
            vt[pl.ds(at, tile, stride=rows), :] = turned
            vt[pl.ds(at + pairs, tile, stride=rows), :] = pltpu.roll(turned, tile // 2, 1)

    left = lax.broadcasted_iota(jnp.int32, (rows, lanes), 1) < lanes // 2
    top = lax.broadcasted_iota(jnp.int32, (rows, lanes), 0) < pairs
    unroll = 256

    def step(i, carry):
        for k in range(unroll):
            f = i * unroll + k
            at = pl.multiple_of(f * rows, 8)
            lhs = vt[pl.ds(at, rows), : 2 * depth].astype(BF16)
            a, b = low_ref[f], high_ref[f]
            straight = jnp.concatenate([a, b], axis=0)
            crossed = jnp.concatenate([a[windows:], -a[:windows], b[windows:], -b[:windows]], axis=0)
            sums = jnp.dot(lhs, jnp.concatenate([straight, crossed], axis=1), preferred_element_type=F32)
            real, imag = sums[:, :lanes], sums[:, lanes:]
            even = jnp.where(top, real, pltpu.roll(imag, pairs, 0))
            odd = jnp.where(top, pltpu.roll(real, pairs, 0), imag)
            st[pl.ds(at, rows), :] = jnp.where(left, even, odd)
        return carry

    lax.fori_loop(0, freqs // unroll, step, 0)


def bins(own, other, turned, after):
    count, windows, width = own.shape
    held = width // 2 * count
    return call(
        bins_kernel,
        (own, other, *turned),
        [VMEM] * 4,
        [((held, LANES), F32)],
        [pltpu.VMEM((held, LANES), F32)],
        10,
        "bins",
        after,
    )[0]


def lags_kernel(st, cos_ref, sin_ref, stay_ref, leave_ref):
    rows, share = stay_ref.shape[:2]
    pairs = rows // 2
    freqs = st.shape[0] // rows
    half = sin_ref.shape[0]
    last_row = lax.broadcasted_iota(jnp.int32, (8, 1), 0) == 7
    for q in range(pairs // 2):
        real, imag = [
            jnp.concatenate(
                [st[pl.ds(i * pairs + 2 * q + k, freqs, stride=rows), :].astype(BF16) for k in (0, 1)], axis=1
            )
            for i in (0, 1)
        ]
        even = jnp.dot(cos_ref[...], real, preferred_element_type=F32)
        odd = jnp.dot(sin_ref[...], imag, preferred_element_type=F32)
        tail = odd[half - 8 :] + jnp.where(last_row, even[half : half + 1], 0.0)
        out = jnp.concatenate([even[:half], odd[: half - 8], tail], axis=0)
        for k in range(2):
            flat = out[:, k * LANES : (k + 1) * LANES].T.astype(BF16)
            for s in range(2):
                at = 2 * share * s
                stay_ref[4 * q + 2 * k + s] = flat[at : at + share]
                leave_ref[4 * q + 2 * k + s] = flat[at + share : at + 2 * share]


def lags(share, rows, sums, tables, after):
    shape = (rows, share, LAGS)
    return call(lags_kernel, (sums, *tables), [VMEM] * 3, [(shape, BF16)] * 2, [], 10, "lags", after)


def unfold_kernel(blocks, starts, sources, *refs):
    ins, mix_ref, outs = refs[: 2 * len(starts)], refs[2 * len(starts)], refs[2 * len(starts) + 1 :]
    held = outs[-1]
    chans, lags = ins[0].shape[1:]
    pitch = sources + 8
    for k, start in enumerate(starts):
        rows = ins[2 * k].shape[0]
        total = jnp.zeros((rows * chans, lags), F32)
        for ref in ins[2 * k : 2 * k + 2]:
            flat = ref[...].reshape(rows * chans, lags)
            total = total + jnp.dot(flat, mix_ref[...], preferred_element_type=F32)
        for r in range(rows):
            at = source_row(blocks, start + r, sources)
            for j in range(lags // LANES):
                lanes = slice(j * LANES, (j + 1) * LANES)
                held[j, pl.ds(at, chans, stride=pitch), :] = total[r * chans : (r + 1) * chans, lanes]
    if len(outs) == 3:
        out_ref = outs[1]
        for c in range(chans):
            for j in range(lags // LANES):
                lanes = slice(j * LANES, (j + 1) * LANES)
                out_ref[c, :, lanes] = held[j, c * pitch : c * pitch + sources, :].astype(BF16)


def unfold(blocks, starts, sources, ins, mix, earlier, after):
    chans, lags = ins[0].shape[1:]
    held = ((lags // LANES, chans * (sources + 8), LANES), F32)
    outs = [((chans, sources, lags), BF16), held] if earlier else [held]
    count = len(ins) + 1
    return call(
        functools.partial(unfold_kernel, blocks, starts, sources),
        (*ins, mix, *earlier),
        [VMEM] * (count + len(earlier)),
        outs,
        [],
        16,
        "unfold",
        after,
        {count: 1} if earlier else None,
    )[0]


def meet_x(keep, send, after):
    return add_parts(keep, lax.ppermute(send, "chan", xor_pairs(8, 1)), after)


def over_z(arrays):
    return [lax.ppermute(array, "chan", xor_pairs(8, 2 * p)) for p, array in zip((1, 2, 3), arrays)]


def over_x(array):
    return lax.ppermute(array, "chan", xor_pairs(8, 1))


def lag_tables(freqs, windows):
    half = LAGS // 2
    f = np.arange(freqs)[None, :]
    scale = np.where(f == 0, 1.0, 2.0) * 0.25 / math.sqrt(freqs * windows)
    u = np.arange(half + 16)[:, None]
    cos = np.where(u <= half, scale * np.cos(math.pi * (f * u % (2 * freqs)) / freqs), 0.0)
    u = np.arange(1, half + 1)[:, None]
    sin = -scale * np.sin(math.pi * (f * u % (2 * freqs)) / freqs) * np.where(u == half, -1.0, 1.0)
    return jnp.asarray(cos.astype(ml_dtypes.bfloat16)), jnp.asarray(sin.astype(ml_dtypes.bfloat16))


def lag_mix():
    half = LAGS // 2
    mix = np.zeros((LAGS, LAGS))
    u = np.arange(half)
    mix[u, half + u] = 1
    u = np.arange(1, half)
    mix[u, half - u] = 1
    mix[half - 1 + u, half + u] = 1
    mix[half - 1 + u, half - u] = -1
    mix[LAGS - 1, 0] = 1
    return jnp.asarray(mix.astype(ml_dtypes.bfloat16))


def on_device(blocks, parts, spectra, valid, sources):
    windows, chans, width = spectra.shape
    freqs = width // 2
    forward = [(i, (i + 1) % blocks) for i in range(blocks)]
    backward = [(b, a) for a, b in forward]
    first, last = rim(spectra)
    low = lax.ppermute(last, "chan", forward)
    high = lax.ppermute(first, "chan", backward)
    white, band, edge_sums, raw = whiten(spectra)
    *picks, edge = edges(blocks, chans, valid, sources, low, high, white, band, edge_sums, raw)
    tables = lag_tables(freqs, windows)
    mix = lag_mix()

    def near(array):
        return lax.ppermute(array, "win", xor_pairs(parts, 1))

    def far(array):
        return lax.ppermute(array, "win", xor_pairs(parts, 2))

    made = {}
    ends = []

    def after(name):
        return [made[key] for key in AFTER.get(name, ()) if key in made]

    def swap(name, rows):
        made[name] = rows
        made[name + "_near"] = near(rows)

    def put(i, name):
        made[f"sums{i}"] = bins(made[name], made[name + "_near"], (made["turned0"], made["turned1"]), after(f"bins{i}"))

    def transform(i):
        sums = made[f"sums{i}"]
        stay, leave = lags(chans // parts, sums.shape[0] // freqs, sums, tables, after(f"lags{i}"))
        made[f"leave{i}"] = leave
        made[f"far{i}"] = far(leave)
        ends.extend([stay, made[f"far{i}"]])

    def turn_halves():
        keep, send = halve(parts, white, edge, chans, after("halve"))
        made["turned0"], made["turned1"] = turn(keep), turn(near(send))

    if blocks == 8:
        pieces_a = meet_x(picks[0], picks[1], ())
        pieces_b = meet_x(picks[2], picks[3], ())
        made["pieces_a"] = pieces_a[0]
        turn_halves()
        sent = own_first([pieces_a[0]] + over_z(pieces_a[1:]), pieces_b[1:], after("own_first"))
        came = over_z(sent)
        rows = pieces_b[0].shape[0]
        swap("mine_a", gather((sent[0], *came), rows, after("gather_a")))
        swap("theirs_a", over_x(made["mine_a"]))
        made["own_b"] = own_b = part(came, pieces_b[0], after("part"))
        others = over_z([own_b] * 3)
        made["other0"], made["other1"], made["other2"] = others
        put(0, "mine_a")
        transform(0)
        swap("mine_b", gather((own_b, *others), rows, after("gather")))
        swap("theirs_b", over_x(made["mine_b"]))
    else:
        turn_halves()
        for name, pick in zip(("mine_a", "theirs_a", "mine_b", "theirs_b"), picks):
            swap(name, lax.psum(pick, "chan"))
        put(0, "mine_a")
        transform(0)
    for i, name in ((1, "theirs_a"), (2, "mine_b"), (3, "theirs_b")):
        put(i, name)
        transform(i)
    count = sources.shape[0]
    starts = [k * count // 4 for k in range(4)]
    held = unfold(blocks, starts[:3], count, ends[:6], mix, (), after("end0"))
    return unfold(blocks, starts[3:], count, ends[6:], mix, (held,), after("end1"))


def solution(mesh):
    return jax.shard_map(
        functools.partial(on_device, mesh.shape["chan"], mesh.shape["win"]),
        mesh=mesh,
        in_specs=(P("win", "chan", None), P("win"), P()),
        out_specs=P(("chan", "win"), None, None),
        check_vma=False,
    )
```

```python
import functools
import math

import jax
import jax.numpy as jnp
import ml_dtypes
import numpy as np
from jax import lax
from jax.experimental import pallas as pl
from jax.experimental.pallas import tpu as pltpu
from jax.sharding import PartitionSpec as P

LAGS = 512
SMOOTH = 21
EPSILON = 1e-06
CHUNKS = 2
LANES = 128
AFTER = {
    "halve": ("pieces_a",),
    "own_first": ("turned0",),
    "gather_a": ("turned1",),
    "lags3": ("far2", "sums1"),
    "gather": ("leave0", "mine_a_near", "other0", "own_b", "theirs_a"),
    "bins3": ("leave1", "sums1", "sums2", "theirs_b", "theirs_b_near"),
    "lags1": ("far0", "other2"),
    "end0": ("leave1", "leave2", "sums1", "theirs_b"),
    "bins1": ("mine_b", "other0", "theirs_b"),
    "part": ("pieces_a",),
    "lags0": ("mine_a", "other0", "other1", "sums0", "turned1"),
    "lags2": ("leave0",),
}
F32 = jnp.float32
BF16 = jnp.bfloat16
MIB = 1024 * 1024
SMEM = pl.BlockSpec(memory_space=pltpu.SMEM)
VMEM = pl.BlockSpec(memory_space=pltpu.VMEM)
ANY = pl.BlockSpec(memory_space=pl.ANY)
HBM = pl.BlockSpec(memory_space=pltpu.HBM)


def call(kernel, ins, in_specs, outs, scratch, limit, name, after=(), aliases=None):
    count = len(ins)

    def body(*refs):
        kernel(*refs[:count], *refs[count + len(after) :])

    return pl.pallas_call(
        body,
        in_specs=[*in_specs] + [ANY] * len(after),
        out_specs=[VMEM] * len(outs),
        out_shape=[jax.ShapeDtypeStruct(shape, dtype) for shape, dtype in outs],
        scratch_shapes=scratch,
        input_output_aliases=aliases or {},
        compiler_params=pltpu.CompilerParams(vmem_limit_bytes=limit * MIB),
        cost_estimate=pl.CostEstimate(flops=0, bytes_accessed=16, transcendentals=0),
        name=name,
    )(*ins, *after)


def xor_pairs(count, mask):
    return [(i, i ^ mask) for i in range(count)]


def place(blocks):
    if blocks != 8:
        return 0, 0
    at = lax.axis_index("chan")
    return at % 2, at // 2


def source_at(blocks, r, per_chunk):
    x, z = place(blocks)
    quarter = per_chunk // 8
    chunk, r = divmod(r, per_chunk)
    half, r = divmod(r, 4 * quarter)
    part, i = divmod(r, quarter)
    return chunk * per_chunk + (x ^ half) * 4 * quarter + (z ^ part) * quarter + i


def source_row(blocks, r, count):
    per_chunk = count // CHUNKS
    return r // per_chunk * per_chunk + source_at(blocks, r % per_chunk, per_chunk)


def amplitude(values):
    freqs = values.shape[-1] // 2
    real, imag = values[:, :freqs], values[:, freqs:]
    square = real * real + imag * imag
    return square * lax.rsqrt(jnp.maximum(square, 1e-36))


def bin_share(freqs):
    f = lax.broadcasted_iota(jnp.int32, (1, freqs), 1)
    entries = jnp.minimum(f, SMOOTH) + jnp.minimum(freqs - 1 - f, SMOOTH) + 1
    return 1.0 / (3.0 * entries.astype(F32))


def inverse_divisor(triple, band, share):
    divisor = jnp.dot(triple, band, preferred_element_type=F32) * share + EPSILON
    near = pl.reciprocal(divisor, approx=True)
    return near * (2.0 - divisor * near)


def rim_kernel(spec_ref, first_ref, last_ref):
    windows, chans, _ = spec_ref.shape
    for w in range(windows):
        first_ref[w] = spec_ref[w, :16].astype(F32)[:1].astype(BF16)
        last_ref[w] = spec_ref[w, chans - 16 :].astype(F32)[15:].astype(BF16)


def rim(spectra):
    windows, _, width = spectra.shape
    return call(rim_kernel, (spectra,), [VMEM], [((windows, 1, width), BF16)] * 2, [], 8, "rim")


def whiten_kernel(spec_ref, white_ref, band, part_ref, raw_ref, buf, tri, inv, sems):
    windows, chans, width = buf.shape
    freqs = width // 2
    pitch = chans + 8
    together = tri.shape[0] // chans

    def fetch(w):
        return pltpu.make_async_copy(spec_ref.at[w], buf.at[w], sems.at[w])

    for w in range(windows):
        fetch(w).start()
    row = lax.broadcasted_iota(jnp.int32, (freqs, freqs), 0)
    col = lax.broadcasted_iota(jnp.int32, (freqs, freqs), 1)
    band[...] = jnp.where(jnp.abs(row - col) <= SMOOTH, 1.0, 0.0).astype(BF16)
    share = bin_share(freqs)

    def some(i, carry):
        for k in range(together):
            w = i * together + k
            fetch(w).wait()
            values = buf[w].astype(F32)
            magnitude = amplitude(values)
            triple = pltpu.roll(magnitude, 1, 0) + magnitude + pltpu.roll(magnitude, chans - 1, 0)
            tri[k * chans : (k + 1) * chans, :] = triple.astype(BF16)
            part_ref[0, pl.ds(w, 1), :] = magnitude[0:1] + magnitude[1:2]
            part_ref[1, pl.ds(w, 1), :] = magnitude[chans - 2 : chans - 1] + magnitude[chans - 1 :]
            raw_ref[0, pl.ds(w, 1), :] = values[0:1]
            raw_ref[1, pl.ds(w, 1), :] = values[chans - 1 :]
        inv[...] = inverse_divisor(tri[...], band[...], share)
        for k in range(together):
            w = i * together + k
            at = pl.multiple_of(w * pitch, 8)
            for j in range(width // LANES):
                values = buf[w, :, j * LANES : (j + 1) * LANES].astype(F32)
                first = j * LANES % freqs
                factor = inv[k * chans : (k + 1) * chans, first : first + LANES]
                white_ref[j, pl.ds(at, chans), :] = values * factor
        return carry

    lax.fori_loop(0, windows // together, some, 0)


def whiten(spectra):
    windows, chans, width = spectra.shape
    freqs = width // 2
    together = 4
    return call(
        whiten_kernel,
        (spectra,),
        [HBM],
        [
            ((width // LANES, (windows + 1) * (chans + 8), LANES), F32),
            ((freqs, freqs), BF16),
            ((2, windows, freqs), F32),
            ((2, windows, width), F32),
        ],
        [
            pltpu.VMEM(spectra.shape, BF16),
            pltpu.VMEM((together * chans, freqs), BF16),
            pltpu.VMEM((together * chans, freqs), F32),
            pltpu.SemaphoreType.DMA((windows,)),
        ],
        28,
        "whiten",
    )


def edges_kernel(blocks, chans, src_ref, valid_ref, low_ref, high_ref, white_ref, band, part_ref, raw_ref, *outs):
    picks, edge_ref = outs[:-1], outs[-1]
    windows, width = raw_ref.shape[1:]
    freqs = width // 2
    sources = src_ref.shape[0]
    pitch = chans + 8
    share = bin_share(freqs)
    row = lax.broadcasted_iota(jnp.int32, (windows, 1), 0)
    valid = jnp.zeros((windows, 1), F32)
    for w in range(windows):
        valid = valid + jnp.where(row == w, valid_ref[w].astype(F32), 0.0)
    for k, ref in enumerate((low_ref, high_ref)):
        beside = jnp.concatenate([ref[w] for w in range(windows)], axis=0).astype(F32)
        triple = (part_ref[k] + amplitude(beside)).astype(BF16)
        inverse = inverse_divisor(triple, band[...], share)
        edge_ref[k] = raw_ref[k] * jnp.concatenate([inverse, inverse], axis=1)
    offset = lax.axis_index("chan") * chans
    rows = picks[0].shape[0]
    for r in range(sources):
        at = src_ref[source_at(blocks, r, sources // CHUNKS)] - offset
        inner = valid * ((at > 0) & (at < chans - 1)).astype(F32)
        first = valid * (at == 0).astype(F32)
        last = valid * (at == chans - 1).astype(F32)
        row_at = jnp.clip(at, 0, chans - 1)
        for j in range(width // LANES):
            lanes = slice(j * LANES, (j + 1) * LANES)
            value = inner * white_ref[j, pl.ds(row_at, windows, stride=pitch), :]
            value = value + first * edge_ref[0, :, lanes] + last * edge_ref[1, :, lanes]
            picks[r // rows][r % rows, :, lanes] = value.astype(BF16)


def edges(blocks, chans, valid, sources, low, high, white, band, part, raw):
    _, windows, width = raw.shape
    rows = sources.shape[0] // CHUNKS // 2
    return call(
        functools.partial(edges_kernel, blocks, chans),
        (sources, valid, low, high, white, band, part, raw),
        [SMEM, SMEM] + [VMEM] * 6,
        [((rows, windows, width), BF16)] * (2 * CHUNKS) + [(raw.shape, F32)],
        [],
        8,
        "edges",
    )


def halve_kernel(white_ref, edge_ref, keep_ref, send_ref):
    windows, chans, width = keep_ref.shape
    share = chans // 2
    pitch = white_ref.shape[1] // (windows + 1)
    blocks = pitch // share
    me = lax.axis_index("win")
    row = lax.broadcasted_iota(jnp.int32, (8, LANES), 0)

    for w in range(windows):
        for out, first in ((keep_ref, me), (send_ref, me ^ 1)):
            for q in range(2):
                block = first ^ (2 * q)
                at = pl.multiple_of(w * pitch + block * share, 8)
                for j in range(width // LANES):
                    lanes = slice(j * LANES, (j + 1) * LANES)
                    body = white_ref[j, pl.ds(at, share), :]
                    top = jnp.where((row == 0) & (block == 0), edge_ref[0, w : w + 1, lanes], body[:8])
                    low = jnp.where((row == 7) & (block == blocks - 1), edge_ref[1, w : w + 1, lanes], body[share - 8 :])
                    body = jnp.concatenate([top, body[8 : share - 8], low], axis=0)
                    out[w, q * share : (q + 1) * share, lanes] = body.astype(BF16)


def halve(parts, white, edge, chans, after):
    _, windows, width = edge.shape
    shape = (windows, 2 * chans // parts, width)
    return call(halve_kernel, (white, edge), [VMEM] * 2, [(shape, BF16)] * 2, [], 8, "halve", after)


def turn_kernel(white_ref, out_ref, held):
    windows, chans, width = white_ref.shape
    tile = LANES
    pitch = 2 * windows + 8

    def block(b, carry):
        for w in range(windows):
            for half in range(2):
                at = pl.multiple_of(half * (width // 2) + b * tile, tile)
                body = white_ref[w, :, pl.ds(at, tile)].astype(F32)
                held[pl.ds(half * windows + w, tile, stride=pitch), :] = jnp.concatenate([body, body], axis=0).T
        for f in range(tile):
            out_ref[b * tile + f] = held[f * pitch : f * pitch + 2 * windows, :].astype(BF16)
        return carry

    lax.fori_loop(0, width // 2 // tile, block, 0)


def turn(white):
    windows, chans, width = white.shape
    return call(
        turn_kernel,
        (white,),
        [VMEM],
        [((width // 2, 2 * windows, 2 * chans), BF16)],
        [pltpu.VMEM((LANES * (2 * windows + 8), LANES), F32)],
        8,
        "turn",
    )[0]


def add_parts_kernel(keep_ref, came_ref, *outs):
    rows = outs[0].shape[0]
    for p, out in enumerate(outs):
        out[...] = keep_ref[p * rows : (p + 1) * rows] + came_ref[p * rows : (p + 1) * rows]


def add_parts(keep, came, after):
    rows, windows, width = keep.shape
    shape = (rows // 4, windows, width)
    return call(add_parts_kernel, (keep, came), [VMEM] * 2, [(shape, BF16)] * 4, [], 8, "add_parts", after)


def own_first_kernel(a_ref, b_ref, c_ref, d_ref, *refs):
    nexts, outs = refs[:3], refs[3:]
    rows = a_ref.shape[0]
    own = a_ref[...] + b_ref[...] + c_ref[...] + d_ref[...]
    for ref, out in zip(nexts, outs):
        out[:rows] = own
        out[rows:] = ref[...]


def own_first(pieces, nexts, after):
    rows, windows, width = pieces[0].shape
    return call(
        own_first_kernel,
        (*pieces, *nexts),
        [VMEM] * 7,
        [((2 * rows, windows, width), BF16)] * 3,
        [],
        8,
        "own_first",
        after,
    )


def gather_kernel(sent_ref, b_ref, c_ref, d_ref, mine_ref):
    rows = mine_ref.shape[0] // 4
    for p, ref in enumerate((sent_ref, b_ref, c_ref, d_ref)):
        mine_ref[p * rows : (p + 1) * rows] = ref[:rows]


def gather(parts_by_z, rows, after=()):
    shape = (4 * rows, *parts_by_z[0].shape[1:])
    return call(gather_kernel, parts_by_z, [VMEM] * 4, [(shape, BF16)], [], 8, "gather", after)[0]


def part_kernel(b_ref, c_ref, d_ref, piece_ref, own_ref):
    rows = piece_ref.shape[0]
    own_ref[...] = piece_ref[...] + b_ref[rows:] + c_ref[rows:] + d_ref[rows:]


def part(came, piece, after=()):
    return call(part_kernel, (*came, piece), [VMEM] * 4, [(piece.shape, BF16)], [], 8, "part", after)[0]


def bins_kernel(own_ref, other_ref, low_ref, high_ref, st, vt):
    rows, windows, width = own_ref.shape
    depth, lanes = low_ref.shape[1:]
    freqs = width // 2
    tile = LANES
    pairs = rows // 2
    for p in range(pairs):
        pieces = []
        for s in (2 * p, 2 * p + 1):
            for ref in (own_ref, other_ref):
                v = ref[s].astype(F32)
                pieces += [v[:, :freqs], v[:, freqs:]]
        stack = jnp.concatenate(pieces, axis=0)
        for j in range(freqs // tile):
            turned = stack[:, j * tile : (j + 1) * tile].T
            at = j * tile * rows + p
            vt[pl.ds(at, tile, stride=rows), :] = turned
            vt[pl.ds(at + pairs, tile, stride=rows), :] = pltpu.roll(turned, tile // 2, 1)

    left = lax.broadcasted_iota(jnp.int32, (rows, lanes), 1) < lanes // 2
    top = lax.broadcasted_iota(jnp.int32, (rows, lanes), 0) < pairs
    unroll = 256

    def step(i, carry):
        for k in range(unroll):
            f = i * unroll + k
            at = pl.multiple_of(f * rows, 8)
            lhs = vt[pl.ds(at, rows), : 2 * depth].astype(BF16)
            a, b = low_ref[f], high_ref[f]
            straight = jnp.concatenate([a, b], axis=0)
            crossed = jnp.concatenate([a[windows:], -a[:windows], b[windows:], -b[:windows]], axis=0)
            sums = jnp.dot(lhs, jnp.concatenate([straight, crossed], axis=1), preferred_element_type=F32)
            real, imag = sums[:, :lanes], sums[:, lanes:]
            even = jnp.where(top, real, pltpu.roll(imag, pairs, 0))
            odd = jnp.where(top, pltpu.roll(real, pairs, 0), imag)
            st[pl.ds(at, rows), :] = jnp.where(left, even, odd)
        return carry

    lax.fori_loop(0, freqs // unroll, step, 0)


def bins(own, other, turned, after):
    count, windows, width = own.shape
    held = width // 2 * count
    return call(
        bins_kernel,
        (own, other, *turned),
        [VMEM] * 4,
        [((held, LANES), F32)],
        [pltpu.VMEM((held, LANES), F32)],
        10,
        "bins",
        after,
    )[0]


def lags_kernel(st, cos_ref, sin_ref, stay_ref, leave_ref):
    rows, share = stay_ref.shape[:2]
    pairs = rows // 2
    freqs = st.shape[0] // rows
    half = sin_ref.shape[0]
    last_row = lax.broadcasted_iota(jnp.int32, (8, 1), 0) == 7
    for q in range(pairs // 2):
        real, imag = [
            jnp.concatenate(
                [st[pl.ds(i * pairs + 2 * q + k, freqs, stride=rows), :].astype(BF16) for k in (0, 1)], axis=1
            )
            for i in (0, 1)
        ]
        even = jnp.dot(cos_ref[...], real, preferred_element_type=F32)
        odd = jnp.dot(sin_ref[...], imag, preferred_element_type=F32)
        tail = odd[half - 8 :] + jnp.where(last_row, even[half : half + 1], 0.0)
        out = jnp.concatenate([even[:half], odd[: half - 8], tail], axis=0)
        for k in range(2):
            flat = out[:, k * LANES : (k + 1) * LANES].T.astype(BF16)
            for s in range(2):
                at = 2 * share * s
                stay_ref[4 * q + 2 * k + s] = flat[at : at + share]
                leave_ref[4 * q + 2 * k + s] = flat[at + share : at + 2 * share]


def lags(share, rows, sums, tables, after):
    shape = (rows, share, LAGS)
    return call(lags_kernel, (sums, *tables), [VMEM] * 3, [(shape, BF16)] * 2, [], 10, "lags", after)


def unfold_kernel(blocks, starts, sources, *refs):
    ins, mix_ref, outs = refs[: 2 * len(starts)], refs[2 * len(starts)], refs[2 * len(starts) + 1 :]
    held = outs[-1]
    chans, lags = ins[0].shape[1:]
    pitch = sources + 8
    for k, start in enumerate(starts):
        rows = ins[2 * k].shape[0]
        total = jnp.zeros((rows * chans, lags), F32)
        for ref in ins[2 * k : 2 * k + 2]:
            flat = ref[...].reshape(rows * chans, lags)
            total = total + jnp.dot(flat, mix_ref[...], preferred_element_type=F32)
        for r in range(rows):
            at = source_row(blocks, start + r, sources)
            for j in range(lags // LANES):
                lanes = slice(j * LANES, (j + 1) * LANES)
                held[j, pl.ds(at, chans, stride=pitch), :] = total[r * chans : (r + 1) * chans, lanes]
    if len(outs) == 3:
        out_ref = outs[1]
        for c in range(chans):
            for j in range(lags // LANES):
                lanes = slice(j * LANES, (j + 1) * LANES)
                out_ref[c, :, lanes] = held[j, c * pitch : c * pitch + sources, :].astype(BF16)


def unfold(blocks, starts, sources, ins, mix, earlier, after):
    chans, lags = ins[0].shape[1:]
    held = ((lags // LANES, (chans + 1) * (sources + 8), LANES), F32)
    outs = [((chans, sources, lags), BF16), held] if earlier else [held]
    count = len(ins) + 1
    return call(
        functools.partial(unfold_kernel, blocks, starts, sources),
        (*ins, mix, *earlier),
        [VMEM] * (count + len(earlier)),
        outs,
        [],
        16,
        "unfold",
        after,
        {count: 1} if earlier else None,
    )[0]


def meet_x(keep, send, after):
    return add_parts(keep, lax.ppermute(send, "chan", xor_pairs(8, 1)), after)


def over_z(arrays):
    return [lax.ppermute(array, "chan", xor_pairs(8, 2 * p)) for p, array in zip((1, 2, 3), arrays)]


def over_x(array):
    return lax.ppermute(array, "chan", xor_pairs(8, 1))


def lag_tables(freqs, windows):
    half = LAGS // 2
    f = np.arange(freqs)[None, :]
    scale = np.where(f == 0, 1.0, 2.0) * 0.25 / math.sqrt(freqs * windows)
    u = np.arange(half + 16)[:, None]
    cos = np.where(u <= half, scale * np.cos(math.pi * (f * u % (2 * freqs)) / freqs), 0.0)
    u = np.arange(1, half + 1)[:, None]
    sin = -scale * np.sin(math.pi * (f * u % (2 * freqs)) / freqs) * np.where(u == half, -1.0, 1.0)
    return jnp.asarray(cos.astype(ml_dtypes.bfloat16)), jnp.asarray(sin.astype(ml_dtypes.bfloat16))


def lag_mix():
    half = LAGS // 2
    mix = np.zeros((LAGS, LAGS))
    u = np.arange(half)
    mix[u, half + u] = 1
    u = np.arange(1, half)
    mix[u, half - u] = 1
    mix[half - 1 + u, half + u] = 1
    mix[half - 1 + u, half - u] = -1
    mix[LAGS - 1, 0] = 1
    return jnp.asarray(mix.astype(ml_dtypes.bfloat16))


def on_device(blocks, parts, spectra, valid, sources):
    windows, chans, width = spectra.shape
    freqs = width // 2
    forward = [(i, (i + 1) % blocks) for i in range(blocks)]
    backward = [(b, a) for a, b in forward]
    first, last = rim(spectra)
    low = lax.ppermute(last, "chan", forward)
    high = lax.ppermute(first, "chan", backward)
    white, band, edge_sums, raw = whiten(spectra)
    *picks, edge = edges(blocks, chans, valid, sources, low, high, white, band, edge_sums, raw)
    tables = lag_tables(freqs, windows)
    mix = lag_mix()

    def near(array):
        return lax.ppermute(array, "win", xor_pairs(parts, 1))

    def far(array):
        return lax.ppermute(array, "win", xor_pairs(parts, 2))

    made = {}
    ends = []

    def after(name):
        return [made[key] for key in AFTER.get(name, ()) if key in made]

    def swap(name, rows):
        made[name] = rows
        made[name + "_near"] = near(rows)

    def put(i, name):
        made[f"sums{i}"] = bins(made[name], made[name + "_near"], (made["turned0"], made["turned1"]), after(f"bins{i}"))

    def transform(i):
        sums = made[f"sums{i}"]
        stay, leave = lags(chans // parts, sums.shape[0] // freqs, sums, tables, after(f"lags{i}"))
        made[f"leave{i}"] = leave
        made[f"far{i}"] = far(leave)
        ends.extend([stay, made[f"far{i}"]])

    def turn_halves():
        keep, send = halve(parts, white, edge, chans, after("halve"))
        made["turned0"], made["turned1"] = turn(keep), turn(near(send))

    if blocks == 8:
        pieces_a = meet_x(picks[0], picks[1], ())
        pieces_b = meet_x(picks[2], picks[3], ())
        made["pieces_a"] = pieces_a[0]
        turn_halves()
        sent = own_first([pieces_a[0]] + over_z(pieces_a[1:]), pieces_b[1:], after("own_first"))
        came = over_z(sent)
        rows = pieces_b[0].shape[0]
        swap("mine_a", gather((sent[0], *came), rows, after("gather_a")))
        swap("theirs_a", over_x(made["mine_a"]))
        made["own_b"] = own_b = part(came, pieces_b[0], after("part"))
        others = over_z([own_b] * 3)
        made["other0"], made["other1"], made["other2"] = others
        put(0, "mine_a")
        transform(0)
        swap("mine_b", gather((own_b, *others), rows, after("gather")))
        swap("theirs_b", over_x(made["mine_b"]))
    else:
        turn_halves()
        for name, pick in zip(("mine_a", "theirs_a", "mine_b", "theirs_b"), picks):
            swap(name, lax.psum(pick, "chan"))
        put(0, "mine_a")
        transform(0)
    for i, name in ((1, "theirs_a"), (2, "mine_b"), (3, "theirs_b")):
        put(i, name)
        transform(i)
    count = sources.shape[0]
    starts = [k * count // 4 for k in range(4)]
    held = unfold(blocks, starts[:3], count, ends[:6], mix, (), after("end0"))
    return unfold(blocks, starts[3:], count, ends[6:], mix, (held,), after("end1"))


def solution(mesh):
    return jax.shard_map(
        functools.partial(on_device, mesh.shape["chan"], mesh.shape["win"]),
        mesh=mesh,
        in_specs=(P("win", "chan", None), P("win"), P()),
        out_specs=P(("chan", "win"), None, None),
        check_vma=False,
    )
```
